256 devices in a mesh: wall: 8 (over x, core), stream: 32 (over z, y).
Axes of the slice: x: 4, y: 4, z: 8, core: 2. Of those that a mesh axis runs over, the one named last changes fastest.
Arguments:
- forcing: float32 [16, 16, 64, 320], P(None, 'wall', 'stream'), may hold values from -72 to 72
- diag_blocks: float32 [16, 64, 320, 320], P('wall', 'stream'), may hold values from -0.04472136 to 2.0447214
- coupling: float32 [4, 16, 64, 320, 320], P(None, 'wall', 'stream'), may hold values from -0.109375 to 0.109375
Outputs:
- solution: float32 [16, 16, 64, 320], P(None, 'wall', 'stream')
- residual: float32 [16, 16, 64, 320], P(None, 'wall', 'stream')
The draws below stay inside these ranges and needn't reach their ends.
All inputs are finite; a program needn't handle non-finite values.
Results may differ from the reference program's by a relative error of at most 0.0003.
Values sent between devices are 32-bit elements; how exact they have to be, the bound alone decides.
No kernel may reach another device: no remote copies, remote signals or barrier semaphores. Data moves between devices by JAX's collectives and lax.ppermute only.
A program may use at most 64 MiB of HBM per device.

```python
import math
import jax
import jax.numpy as jnp
from jax import lax

ROWS = 320
BLOCK = 16
STEPS = 4
CYCLES = 2
PANEL = 80
NW = 16
NS = 64


def draw_forcing(key, part):
    key = jax.random.fold_in(key, 11)
    base_key, element_key, column_key = jax.random.split(key, 3)
    shape = (BLOCK, NW, NS, ROWS)
    base = jnp.clip(jax.random.normal(base_key, shape, jnp.float32), -4.0, 4.0)
    element_scale = jnp.exp(jax.random.uniform(element_key, (1, NW, NS, 1), jnp.float32, math.log(0.2), math.log(2.0)))
    column_scale = jnp.exp(jax.random.uniform(column_key, (BLOCK, 1, 1, 1), jnp.float32, math.log(0.3), math.log(3.0)))
    profile = jnp.exp(math.log(3.0) * jnp.arange(NS, dtype=jnp.float32) / (NS - 1))
    return base * element_scale * column_scale * profile[None, None, :, None]


def draw_diag_blocks(key, part):
    key = jax.random.fold_in(key, 12)
    level_key, noise_key = jax.random.split(key, 2)
    levels = jax.random.uniform(level_key, (NW, NS, ROWS), jnp.float32, 1.0, 2.0)
    spread = 0.2 / math.sqrt(ROWS)
    shape = (NW, NS, ROWS, ROWS)
    noise = jnp.clip(jax.random.normal(noise_key, shape, jnp.float32), -4.0, 4.0) * spread
    return noise + levels[..., None] * jnp.eye(ROWS, dtype=jnp.float32)


def block_scale(key, extent, pieces, low, top_value):
    def one(axis_at, shards_of):
        heights = jax.random.uniform(jax.random.fold_in(jax.random.fold_in(key, 6), axis_at), (shards_of,), jnp.float32, low / len(pieces), top_value / len(pieces))
        return jnp.repeat(jnp.exp(heights), extent[axis_at] // shards_of).reshape((-1,) + (1,) * (len(extent) - axis_at - 1))

    level = one(*pieces[0])
    for cut in pieces[1:]:
        level = level * one(*cut)
    return level


def centred(key, dims, width, limit, cuts=(), kind=jnp.bfloat16):
    values = jax.random.normal(key, dims, jnp.float32) * width
    if len(cuts) > 0:
        values = block_scale(key, dims, cuts, -0.22, 0.18) * values
    return jnp.clip(values, min=-limit, max=limit).astype(kind)


def setup_inputs(seed: int = 0) -> dict:
    splits = jax.random.split(jax.random.key(seed), 4)
    forcing = draw_forcing(jax.random.fold_in(splits[3], 71), 0)
    diag_blocks = draw_diag_blocks(jax.random.fold_in(splits[3], 71), 0)
    coupling = centred(splits[2], (4, NW, NS, ROWS, ROWS), (10 * ROWS) ** -0.5, 0.109375, ((1, 8), (2, 32)), jnp.float32)
    return dict(forcing=forcing, diag_blocks=diag_blocks, coupling=coupling)


highest = lax.Precision.HIGHEST
basis_shift = 1.5
basis_scale = 0.8

def operate(vector, diag_blocks, coupling):
    result = jnp.einsum('wsij,bwsj->bwsi', diag_blocks, vector, precision=highest)
    wall_zero = jnp.zeros_like(vector[:, :1])
    stream_zero = jnp.zeros_like(vector[:, :, :1])
    neighbours = (jnp.concatenate([wall_zero, vector[:, :-1]], axis=1), jnp.concatenate([vector[:, 1:], wall_zero], axis=1), jnp.concatenate([stream_zero, vector[:, :, :-1]], axis=2), jnp.concatenate([vector[:, :, 1:], stream_zero], axis=2))
    for face_index in range(4):
        result = result + jnp.einsum('wsij,bwsj->bwsi', coupling[face_index], neighbours[face_index], precision=highest)
    return result

def small_solve(gram_matrix):
    upper_factor = jnp.linalg.cholesky(gram_matrix).T
    inner_width = PANEL - BLOCK
    recurrence = basis_shift * jnp.eye(PANEL, inner_width, dtype=jnp.float32) + basis_scale * jnp.eye(PANEL, inner_width, k=-BLOCK, dtype=jnp.float32)
    projected = jnp.dot(upper_factor, recurrence, precision=highest)
    normal_system = jnp.dot(projected.T, projected, precision=highest)
    target_side = jnp.dot(projected.T, upper_factor[:, :BLOCK], precision=highest)
    lower_factor = jnp.linalg.cholesky(normal_system)
    halfway = lax.linalg.triangular_solve(lower_factor, target_side, left_side=True, lower=True)
    coefficients = lax.linalg.triangular_solve(lower_factor, halfway, left_side=True, lower=True, transpose_a=True)
    update = jnp.dot(recurrence, coefficients, precision=highest)
    return (coefficients, update)

def reference(forcing, diag_blocks, coupling):
    solution = jnp.zeros_like(forcing)
    residual = forcing
    for cycle_index in range(CYCLES):
        blocks = [residual]
        for power_index in range(STEPS):
            newest = (operate(blocks[-1], diag_blocks, coupling) - basis_shift * blocks[-1]) / basis_scale
            blocks.append(newest)
        krylov_basis = jnp.concatenate(blocks, axis=0)
        flattened = krylov_basis.reshape(krylov_basis.shape[0], -1)
        gram_matrix = jnp.dot(flattened, flattened.T, precision=highest)
        coefficients, update = small_solve(gram_matrix)
        inner_width = PANEL - BLOCK
        solution = solution + jnp.einsum('mb,mwsr->bwsr', coefficients, krylov_basis[:inner_width], precision=highest)
        residual = residual - jnp.einsum('mb,mwsr->bwsr', update, krylov_basis, precision=highest)
    return (solution, residual)
```

```python
import jax
import jax.numpy as jnp
from jax import lax
from jax.sharding import PartitionSpec as P

BLOCK = 16
STEPS = 4
CYCLES = 2
PANEL = 80


highest = lax.Precision.HIGHEST
basis_shift = 1.5
basis_scale = 0.8


def shifted(block, axis, step):
    count = lax.axis_size(axis)
    ring = [(i, (i + step) % count) for i in range(count)]
    received = lax.ppermute(block, axis, ring)
    edge = 0 if step == 1 else count - 1
    return jnp.where(lax.axis_index(axis) == edge, 0.0, received)


def operate(vector, diag_blocks, coupling):
    result = jnp.einsum("wsij,bwsj->bwsi", diag_blocks, vector, precision=highest)
    below = shifted(vector[:, -1:], "wall", 1)
    above = shifted(vector[:, :1], "wall", -1)
    before = shifted(vector[:, :, -1:], "stream", 1)
    behind = shifted(vector[:, :, :1], "stream", -1)
    neighbours = (
        jnp.concatenate([below, vector[:, :-1]], axis=1),
        jnp.concatenate([vector[:, 1:], above], axis=1),
        jnp.concatenate([before, vector[:, :, :-1]], axis=2),
        jnp.concatenate([vector[:, :, 1:], behind], axis=2),
    )
    for face_index in range(4):
        result = result + jnp.einsum(
            "wsij,bwsj->bwsi", coupling[face_index], neighbours[face_index], precision=highest
        )
    return result


def groups_by(key):
    found = {}
    for wall in range(8):
        for stream in range(32):
            place = key(wall // 2, wall % 2, stream % 4, stream // 4)
            found.setdefault(place, []).append(wall * 32 + stream)
    return list(found.values())


NEAR = groups_by(lambda x, core, y, z: (y // 2, z))
FAR = groups_by(lambda x, core, y, z: (x, core, y % 2))


def gram_total(partial_value):
    total = jnp.pad(partial_value, ((0, 0), (0, 128 - PANEL)))
    for groups in (NEAR, FAR):
        copies = jnp.broadcast_to(total[None], (16, *total.shape))
        total = jnp.sum(
            lax.all_to_all(copies, ("wall", "stream"), 0, 0, axis_index_groups=groups), axis=0
        )
    return total[:, :PANEL]


def local_gram(left_side, right_side):
    left_flat = left_side.reshape(left_side.shape[0], -1)
    right_flat = right_side.reshape(right_side.shape[0], -1)
    return jnp.dot(left_flat, right_flat.T, precision=highest)


def small_solve(gram_matrix):
    upper_factor = jnp.linalg.cholesky(gram_matrix).T
    inner_width = PANEL - BLOCK
    recurrence = basis_shift * jnp.eye(
        PANEL, inner_width, dtype=jnp.float32
    ) + basis_scale * jnp.eye(PANEL, inner_width, k=-BLOCK, dtype=jnp.float32)
    projected = jnp.dot(upper_factor, recurrence, precision=highest)
    normal_system = jnp.dot(projected.T, projected, precision=highest)
    target_side = jnp.dot(projected.T, upper_factor[:, :BLOCK], precision=highest)
    lower_factor = jnp.linalg.cholesky(normal_system)
    halfway = lax.linalg.triangular_solve(lower_factor, target_side, left_side=True, lower=True)
    coefficients = lax.linalg.triangular_solve(
        lower_factor, halfway, left_side=True, lower=True, transpose_a=True
    )
    update = jnp.dot(recurrence, coefficients, precision=highest)
    return (coefficients, update)


def on_device(forcing, diag_blocks, coupling):
    solution = jnp.zeros_like(forcing)
    residual = forcing
    for cycle_index in range(CYCLES):
        blocks = [residual]
        for power_index in range(STEPS):
            newest = (
                operate(blocks[-1], diag_blocks, coupling) - basis_shift * blocks[-1]
            ) / basis_scale
            blocks.append(newest)
        krylov_basis = jnp.concatenate(blocks, axis=0)
        gram_matrix = gram_total(local_gram(krylov_basis, krylov_basis))
        coefficients, update = small_solve(gram_matrix)
        inner_width = PANEL - BLOCK
        solution = solution + jnp.einsum(
            "mb,mwsr->bwsr", coefficients, krylov_basis[:inner_width], precision=highest
        )
        residual = residual - jnp.einsum("mb,mwsr->bwsr", update, krylov_basis, precision=highest)
    return (solution, residual)


def solution(mesh):
    return jax.shard_map(
        on_device,
        mesh=mesh,
        in_specs=(
            P(None, "wall", "stream", None),
            P("wall", "stream", None, None),
            P(None, "wall", "stream", None, None),
        ),
        out_specs=(P(None, "wall", "stream", None), P(None, "wall", "stream", None)),
        check_vma=False,
    )
```

```python
import jax
import jax.numpy as jnp
from jax import lax
from jax.experimental import pallas as pl
from jax.experimental.pallas import tpu as pltpu
from jax.sharding import PartitionSpec as P

ROWS = 320
BLOCK = 16
STEPS = 4
PANEL = 80
INNER = PANEL - BLOCK
SPAN = 2 * STEPS + 1
basis_shift = 1.5
basis_scale = 0.8

f32 = jnp.float32
bf16 = jnp.bfloat16
highest = lax.Precision.HIGHEST
AXES = ("wall", "stream")
NT = (((1,), (1,)), ((), ()))
VMEM = pl.BlockSpec(memory_space=pltpu.VMEM)
SMEM = pl.BlockSpec(memory_space=pltpu.SMEM)


def groups_by(key):
    found = {}
    for wall in range(8):
        for stream in range(32):
            place = key(wall // 2, wall % 2, stream % 4, stream // 4)
            found.setdefault(place, []).append(wall * 32 + stream)
    return list(found.values())


NEAR = groups_by(lambda x, core, y, z: (y % 2, z))
FAR = groups_by(lambda x, core, y, z: (x, core, y // 2))
COPIES = 16


def call(kernel, name, out_shape, operands, flops, in_specs=None):
    return pl.pallas_call(
        kernel,
        in_specs=in_specs or [VMEM] * len(operands),
        out_specs=jax.tree.map(lambda _: VMEM, out_shape),
        out_shape=out_shape,
        compiler_params=pltpu.CompilerParams(vmem_limit_bytes=16 * 2**20),
        cost_estimate=pl.CostEstimate(flops=flops, bytes_accessed=2**20, transcendentals=0),
        name=name,
    )(*operands)


def shape(*dims, dtype=f32):
    return jax.ShapeDtypeStruct(dims, dtype)


def split(value):
    high = value.astype(bf16)
    return high, (value - high.astype(f32)).astype(bf16)


def prepare_kernel(diag, coupling, local_high, local_low, far_high, far_low):
    element = pl.program_id(0)
    wall, stream = element // 2, element % 2
    row = lax.broadcasted_iota(jnp.int32, (ROWS, ROWS), 0)
    column = lax.broadcasted_iota(jnp.int32, (ROWS, ROWS), 1)

    def store(high, low, at, matrix):
        high_part, low_part = split(matrix * (1.0 / basis_scale))
        high[element, :, at * ROWS : (at + 1) * ROWS] = high_part
        low[element, :, at * ROWS : (at + 1) * ROWS] = low_part

    store(local_high, local_low, 0, diag[0, 0] - jnp.where(row == column, basis_shift, 0.0))
    store(local_high, local_low, 1, coupling[1 - wall, 0, 0])
    store(local_high, local_low, 2, coupling[3 - stream, 0, 0])
    store(far_high, far_low, 0, coupling[wall, 0, 0])
    store(far_high, far_low, 1, coupling[2 + stream, 0, 0])


def prepare(diag_blocks, coupling):
    return pl.pallas_call(
        prepare_kernel,
        grid=(4,),
        in_specs=[
            pl.BlockSpec((1, 1, ROWS, ROWS), lambda e: (e // 2, e % 2, 0, 0)),
            pl.BlockSpec((4, 1, 1, ROWS, ROWS), lambda e: (0, e // 2, e % 2, 0, 0)),
        ],
        out_specs=[VMEM] * 4,
        out_shape=[shape(4, ROWS, 3 * ROWS, dtype=bf16)] * 2
        + [shape(4, ROWS, 2 * ROWS, dtype=bf16)] * 2,
        compiler_params=pltpu.CompilerParams(vmem_limit_bytes=32 * 2**20),
        cost_estimate=pl.CostEstimate(flops=0, bytes_accessed=2**24, transcendentals=0),
        name="prepare",
    )(diag_blocks, coupling)


def times(high, low, sources):
    highs, lows = zip(*[split(source) for source in sources])
    high_source = jnp.concatenate(highs, axis=1)
    both = jnp.concatenate([high_source, jnp.concatenate(lows, axis=1)], axis=0)
    first = lax.dot_general(both, high, NT, preferred_element_type=f32)
    second = lax.dot_general(high_source, low, NT, preferred_element_type=f32)
    return first[:BLOCK] + (first[BLOCK:] + second)


def local_kernel(wall0, wall1, high, low, partial):
    field = (wall0, wall1)
    for w in range(2):
        for s in range(2):
            sources = [field[w][s], field[1 - w][s], field[w][1 - s]]
            partial[w, s] = times(high[2 * w + s], low[2 * w + s], sources)


def far_kernel(inside, partial, below, above, before, behind, high, low, *faces):
    wall_side, stream_side = (below, above), (before, behind)
    for w in range(2):
        for s in range(2):
            sources = [
                jnp.where(inside[w] > 0, wall_side[w][s], 0.0),
                jnp.where(inside[2 + s] > 0, stream_side[s][w], 0.0),
            ]
            value = partial[w, s] + times(high[2 * w + s], low[2 * w + s], sources)
            faces[w][s] = value
            faces[2 + s][w] = value


def start_kernel(forcing, *faces):
    for w in range(2):
        for s in range(2):
            value = forcing[:, w, s, :]
            faces[w][s] = value
            faces[2 + s][w] = value


FACES = [shape(2, BLOCK, ROWS)] * 4


def ring(array, axis, step):
    count = lax.axis_size(axis)
    return lax.ppermute(array, axis, [(i, (i + step) % count) for i in range(count)])


def advance(faces, parts, inside):
    wall0, wall1, stream0, stream1 = faces
    below, above = ring(wall1, "wall", 1), ring(wall0, "wall", -1)
    before, behind = ring(stream1, "stream", 1), ring(stream0, "stream", -1)
    local_high, local_low, far_high, far_low = parts
    partial = call(
        local_kernel, "local", shape(2, 2, BLOCK, ROWS), (wall0, wall1, local_high, local_low), 10**9
    )
    return call(
        far_kernel,
        "far",
        FACES,
        (inside, partial, below, above, before, behind, far_high, far_low),
        10**9,
        in_specs=[SMEM] + [VMEM] * 7,
    )


def pack_gram(panels):
    gram = sum(
        lax.dot_general(p, p, NT, precision=highest, preferred_element_type=f32) for p in panels
    )
    first = jnp.concatenate([gram[:16], gram[48:64, 48:], gram[64:, 64:]], axis=1)
    second = jnp.concatenate([gram[16:32, 16:], gram[32:48, 32:], jnp.zeros((16, 16), f32)], axis=1)
    return jnp.concatenate([first, second], axis=0)


def unpack_gram(packed):
    first, second = packed[:16], packed[16:]
    zeros = lambda width: jnp.zeros((16, width), f32)
    upper = jnp.concatenate(
        [
            jnp.concatenate([first[:, :80], zeros(48)], axis=1),
            jnp.concatenate([zeros(16), second[:, :64], zeros(48)], axis=1),
            jnp.concatenate([zeros(32), second[:, 64:112], zeros(48)], axis=1),
            jnp.concatenate([zeros(48), first[:, 80:112], zeros(48)], axis=1),
            jnp.concatenate([zeros(64), first[:, 112:], zeros(48)], axis=1),
            jnp.zeros((48, 128), f32),
        ],
        axis=0,
    )
    row = lax.broadcasted_iota(jnp.int32, (128, 128), 0) // BLOCK
    column = lax.broadcasted_iota(jnp.int32, (128, 128), 1) // BLOCK
    return jnp.where(row <= column, upper, upper.T)


def small_solve(gram):
    right = basis_shift * gram[:PANEL, :INNER] + basis_scale * gram[:PANEL, BLOCK:PANEL]
    normal = basis_shift * right[:INNER] + basis_scale * right[BLOCK:]
    target = basis_shift * gram[:INNER, :BLOCK] + basis_scale * gram[BLOCK:PANEL, :BLOCK]
    system = jnp.concatenate([normal, target, jnp.zeros((INNER, 48), f32)], axis=1)
    rows = lax.broadcasted_iota(jnp.int32, (INNER, 128), 0)
    group = 4
    for start in range(0, INNER, group):
        columns = [
            jnp.broadcast_to(system[:, start + j : start + j + 1], (INNER, 128))
            for j in range(group)
        ]
        for j in range(group):
            k = start + j
            inverse = 1.0 / columns[j][k : k + 1]
            pivot_row = system[k : k + 1] * inverse
            system = jnp.where(rows == k, pivot_row, system - columns[j] * pivot_row)
            for later in range(j + 1, group):
                scaled = columns[later][k : k + 1] * inverse
                columns[later] = jnp.where(
                    rows == k, scaled, columns[later] - columns[j] * scaled
                )
    coefficients = system[:, INNER:PANEL]
    zero = jnp.zeros((BLOCK, BLOCK), f32)
    update = basis_shift * jnp.concatenate([coefficients, zero], axis=0)
    update = update + basis_scale * jnp.concatenate([zero, coefficients], axis=0)
    return coefficients, update


def transposed(value):
    return value.T


def spread(packed, copies):
    copies[...] = jnp.broadcast_to(packed[None], copies.shape)


def element_panels(powers):
    count = len(powers) // 2
    return [
        jnp.concatenate([powers[2 * j + w][s] for j in range(count)], axis=0)
        for w in range(2)
        for s in range(2)
    ]


def gram_kernel(*refs):
    spread(pack_gram(element_panels(refs[:-1])), refs[-1])


def resum_kernel(received, copies):
    spread(jnp.sum(received[...], axis=0), copies)


def device_sum(copies):
    received = lax.all_to_all(copies, AXES, 0, 0, axis_index_groups=NEAR)
    copies = call(resum_kernel, "resum", shape(COPIES, 32, 128), (received,), 10**6)
    return lax.all_to_all(copies, AXES, 0, 0, axis_index_groups=FAR)


def restart_kernel(received, *refs):
    powers, (solution, basis, copies) = refs[:-3], refs[-3:]
    coefficients, update = small_solve(unpack_gram(jnp.sum(received[...], axis=0)))
    update = -transposed(update)
    width = SPAN * BLOCK
    lines = [
        jnp.concatenate(
            [
                jnp.zeros((BLOCK, BLOCK * j), f32),
                update,
                jnp.zeros((BLOCK, width - PANEL - BLOCK * j), f32),
            ][(0 if j else 1) : (3 if j < STEPS else 2)],
            axis=1,
        )
        for j in range(STEPS + 1)
    ]
    lines.append(
        jnp.concatenate([transposed(coefficients), jnp.zeros((BLOCK, width - INNER), f32)], axis=1)
    )
    weights = jnp.concatenate(lines, axis=0)
    panels = []
    for e, panel in enumerate(element_panels(powers)):
        mixed = jnp.dot(weights, panel, precision=highest, preferred_element_type=f32)
        panels.append(panel[:PANEL] + mixed[:PANEL])
        basis[e] = panels[-1]
        solution[e] = mixed[PANEL:]
    spread(pack_gram(panels), copies)


def finish_kernel(received, solution, basis, solution_out, residual_out):
    coefficients, update = small_solve(unpack_gram(jnp.sum(received[...], axis=0)))
    weights = jnp.concatenate(
        [
            jnp.concatenate([transposed(coefficients), jnp.zeros((BLOCK, BLOCK), f32)], axis=1),
            -transposed(update),
        ],
        axis=0,
    )
    for w in range(2):
        for s in range(2):
            e = 2 * w + s
            panel = basis[e]
            mixed = jnp.dot(weights, panel, precision=highest, preferred_element_type=f32)
            solution_out[:, w, s, :] = solution[e] + mixed[:BLOCK]
            residual_out[:, w, s, :] = panel[:BLOCK] + mixed[BLOCK:]


def on_device(forcing, diag_blocks, coupling):
    wall, stream = lax.axis_index("wall"), lax.axis_index("stream")
    inside = jnp.stack([wall > 0, wall < 7, stream > 0, stream < 31]).astype(jnp.int32)
    faces = call(start_kernel, "start", FACES, (forcing,), 10**6)
    parts = prepare(diag_blocks, coupling)
    powers = [*faces[:2]]
    received = None
    for step in range(2 * STEPS):
        faces = advance(faces, parts, inside)
        powers += faces[:2]
        if step == STEPS - 1:
            copies = call(gram_kernel, "gram", shape(COPIES, 32, 128), powers, 10**7)
            received = device_sum(copies)
    solution, basis, copies = call(
        restart_kernel,
        "restart",
        [shape(4, BLOCK, ROWS), shape(4, PANEL, ROWS), shape(COPIES, 32, 128)],
        (received, *powers),
        10**8,
    )
    return call(
        finish_kernel,
        "finish",
        [shape(BLOCK, 2, 2, ROWS)] * 2,
        (device_sum(copies), solution, basis),
        10**8,
    )


def solution(mesh):
    return jax.shard_map(
        on_device,
        mesh=mesh,
        in_specs=(
            P(None, "wall", "stream", None),
            P("wall", "stream", None, None),
            P(None, "wall", "stream", None, None),
        ),
        out_specs=(P(None, "wall", "stream", None), P(None, "wall", "stream", None)),
        check_vma=False,
    )
```

```python
import functools

import jax
import jax.numpy as jnp
from jax import lax
from jax.experimental import pallas as pl
from jax.experimental.pallas import tpu as pltpu
from jax.sharding import PartitionSpec as P

ROWS = 320
BLOCK = 16
STEPS = 4
PANEL = 80
INNER = PANEL - BLOCK
SPAN = 2 * STEPS + 1
basis_shift = 1.5
basis_scale = 0.8

f32 = jnp.float32
bf16 = jnp.bfloat16
highest = lax.Precision.HIGHEST
AXES = ("wall", "stream")
NT = (((1,), (1,)), ((), ()))
VMEM = pl.BlockSpec(memory_space=pltpu.VMEM)
SMEM = pl.BlockSpec(memory_space=pltpu.SMEM)


def groups_by(key):
    found = {}
    for wall in range(8):
        for stream in range(32):
            place = key(wall // 2, wall % 2, stream % 4, stream // 4)
            found.setdefault(place, []).append(wall * 32 + stream)
    return list(found.values())


PLANE = groups_by(lambda x, core, y, z: (core, z))
DEPTH = groups_by(lambda x, core, y, z: (core, x, y))
SIBLING = [(w * 32 + r, (w ^ 1) * 32 + r) for w in range(8) for r in range(32)]
WIDTH = SPAN * BLOCK
PACKED = 96
GROWTH = 2.0**-4


def call(kernel, name, out_shape, operands, flops, in_specs=None):
    return pl.pallas_call(
        kernel,
        in_specs=in_specs or [VMEM] * len(operands),
        out_specs=jax.tree.map(lambda _: VMEM, out_shape),
        out_shape=out_shape,
        compiler_params=pltpu.CompilerParams(vmem_limit_bytes=8 * 2**20),
        cost_estimate=pl.CostEstimate(flops=flops, bytes_accessed=2**20, transcendentals=0),
        name=name,
    )(*operands)


def shape(*dims, dtype=f32):
    return jax.ShapeDtypeStruct(dims, dtype)


def split(value):
    high = value.astype(bf16)
    return high, (value - high.astype(f32)).astype(bf16)


def prepare_kernel(diag, coupling, local_high, local_low, far_high, far_low):
    element = pl.program_id(0)
    wall, stream = element // 2, element % 2
    row = lax.broadcasted_iota(jnp.int32, (ROWS, ROWS), 0)
    column = lax.broadcasted_iota(jnp.int32, (ROWS, ROWS), 1)

    def store(high, low, at, matrix):
        high_part, low_part = split(matrix * (1.0 / basis_scale))
        high[element, :, at * ROWS : (at + 1) * ROWS] = high_part
        low[element, :, at * ROWS : (at + 1) * ROWS] = low_part

    store(local_high, local_low, 0, diag[0, 0] - jnp.where(row == column, basis_shift, 0.0))
    store(local_high, local_low, 1, coupling[1 - wall, 0, 0])
    store(local_high, local_low, 2, coupling[3 - stream, 0, 0])
    store(far_high, far_low, 0, coupling[wall, 0, 0])
    store(far_high, far_low, 1, coupling[2 + stream, 0, 0])


def prepare(diag_blocks, coupling):
    return pl.pallas_call(
        prepare_kernel,
        grid=(4,),
        in_specs=[
            pl.BlockSpec((1, 1, ROWS, ROWS), lambda e: (e // 2, e % 2, 0, 0)),
            pl.BlockSpec((4, 1, 1, ROWS, ROWS), lambda e: (0, e // 2, e % 2, 0, 0)),
        ],
        out_specs=[VMEM] * 4,
        out_shape=[shape(4, ROWS, 3 * ROWS, dtype=bf16)] * 2
        + [shape(4, ROWS, 2 * ROWS, dtype=bf16)] * 2,
        compiler_params=pltpu.CompilerParams(vmem_limit_bytes=32 * 2**20),
        cost_estimate=pl.CostEstimate(flops=0, bytes_accessed=2**24, transcendentals=0),
        name="prepare",
    )(
        pltpu.with_memory_space_constraint(diag_blocks, pltpu.HBM),
        pltpu.with_memory_space_constraint(coupling, pltpu.HBM),
    )


def times(high, low, sources):
    highs, lows = zip(*[split(source) for source in sources])
    high_source = jnp.concatenate(highs, axis=1)
    both = jnp.concatenate([high_source, jnp.concatenate(lows, axis=1)], axis=0)
    first = lax.dot_general(both, high, NT, preferred_element_type=f32)
    second = lax.dot_general(high_source, low, NT, preferred_element_type=f32)
    return first[:BLOCK] + (first[BLOCK:] + second)


def gram_row(powers):
    panels = element_panels(powers)
    return sum(
        lax.dot_general(
            panel[-BLOCK:], panel, NT, precision=highest, preferred_element_type=f32
        )
        for panel in panels
    )


def local_kernel(high, low, *refs):
    powers, (partial, row) = refs[:-2], refs[-2:]
    field = powers[-2:]
    for w in range(2):
        for s in range(2):
            sources = [field[w][s], field[1 - w][s], field[w][1 - s]]
            partial[w, s] = times(high[2 * w + s], low[2 * w + s], sources)
    row[...] = gram_row(powers)


def far_kernel(scale, inside, partial, below, above, before, behind, high, low, *faces):
    wall_side, stream_side = (below, above), (before, behind)
    for w in range(2):
        for s in range(2):
            sources = [
                jnp.where(inside[w] > 0, wall_side[w][s], 0.0),
                jnp.where(inside[2 + s] > 0, stream_side[s][w], 0.0),
            ]
            value = partial[w, s] + times(high[2 * w + s], low[2 * w + s], sources)
            if scale != 1.0:
                value = value * scale
            faces[w][s] = value
            faces[2 + s][w] = value


def start_kernel(forcing, *faces):
    for w in range(2):
        for s in range(2):
            value = forcing[:, w, s, :]
            faces[w][s] = value
            faces[2 + s][w] = value


FACES = [shape(2, BLOCK, ROWS)] * 4


def ring(array, axis, step):
    count = lax.axis_size(axis)
    return lax.ppermute(array, axis, [(i, (i + step) % count) for i in range(count)])


def advance(faces, powers, parts, inside, scale):
    wall0, wall1, stream0, stream1 = faces
    below, above = ring(wall1, "wall", 1), ring(wall0, "wall", -1)
    before, behind = ring(stream1, "stream", 1), ring(stream0, "stream", -1)
    local_high, local_low, far_high, far_low = parts
    partial, row = call(
        local_kernel,
        "local",
        [shape(2, 2, BLOCK, ROWS), shape(BLOCK, 8 * len(powers))],
        (local_high, local_low, *powers),
        10**9,
    )
    faces = call(
        functools.partial(far_kernel, scale),
        "far",
        FACES,
        (inside, partial, below, above, before, behind, far_high, far_low),
        10**9,
        in_specs=[SMEM] + [VMEM] * 7,
    )
    return faces, row


def pack_kernel(inside, *refs):
    rows, powers, (keep, send) = refs[: SPAN - 1], refs[SPAN - 1 : -2], refs[-2:]
    lines = [row[...] for row in rows] + [gram_row(powers)]
    last = lines[8]
    first_half = jnp.concatenate(
        [last[:, :128], lines[7], jnp.concatenate([lines[6], lines[0]], axis=1)], axis=0
    )
    second_half = jnp.concatenate(
        [
            jnp.concatenate([lines[5], lines[1]], axis=1),
            jnp.concatenate([lines[4], lines[2]], axis=1),
            jnp.concatenate([lines[3], last[:, 128:], jnp.zeros((BLOCK, 48), f32)], axis=1),
        ],
        axis=0,
    )
    core = inside[4] > 0
    keep[...] = jnp.where(core, second_half, first_half)
    send[...] = jnp.where(core, first_half, second_half)


def unpack_gram(first, second):
    lines = [
        first[32:48, 112:],
        second[:16, 96:],
        second[16:32, 80:],
        second[32:48, :64],
        second[16:32, :80],
        second[:16, :96],
        first[32:48, :112],
        first[16:32],
        jnp.concatenate([first[:16], second[32:48, 64:80]], axis=1),
    ]
    lower = jnp.concatenate(
        [
            line
            if line.shape[1] == WIDTH
            else jnp.concatenate([line, jnp.zeros((BLOCK, WIDTH - line.shape[1]), f32)], axis=1)
            for line in lines
        ],
        axis=0,
    )
    row = lax.broadcasted_iota(jnp.int32, (WIDTH, WIDTH), 0) // BLOCK
    column = lax.broadcasted_iota(jnp.int32, (WIDTH, WIDTH), 1) // BLOCK
    return jnp.where(row >= column, lower, lower.T)


def small_solve(gram):
    right = basis_shift * gram[:, :INNER] + basis_scale * gram[:, BLOCK:]
    normal = basis_shift * right[:INNER] + basis_scale * right[BLOCK:]
    target = basis_shift * gram[:INNER, :BLOCK] + basis_scale * gram[BLOCK:, :BLOCK]
    system = jnp.concatenate([normal, target, jnp.zeros((INNER, 48), f32)], axis=1)
    rows = lax.broadcasted_iota(jnp.int32, (INNER, 128), 0)
    group = 4
    for start in range(0, INNER, group):
        columns = [
            jnp.broadcast_to(system[:, start + j : start + j + 1], (INNER, 128))
            for j in range(group)
        ]
        for j in range(group):
            k = start + j
            inverse = 1.0 / columns[j][k : k + 1]
            pivot_row = system[k : k + 1] * inverse
            system = jnp.where(rows == k, pivot_row, system - columns[j] * pivot_row)
            for later in range(j + 1, group):
                scaled = columns[later][k : k + 1] * inverse
                columns[later] = jnp.where(
                    rows == k, scaled, columns[later] - columns[j] * scaled
                )
    coefficients = system[:, INNER:PANEL]
    zero = jnp.zeros((BLOCK, BLOCK), f32)
    update = basis_shift * jnp.concatenate([coefficients, zero], axis=0)
    update = update + basis_scale * jnp.concatenate([zero, coefficients], axis=0)
    return coefficients, update


def element_panels(powers):
    count = len(powers) // 2
    return [
        jnp.concatenate([powers[2 * j + w][s] for j in range(count)], axis=0)
        for w in range(2)
        for s in range(2)
    ]


def add_spread_kernel(own, other, copies):
    copies[...] = jnp.broadcast_to((own[...] + other[...])[None], copies.shape)


def sum_spread_kernel(received, copies):
    copies[...] = jnp.broadcast_to(jnp.sum(received[...], axis=0)[None], copies.shape)


def sum_kernel(received, total):
    total[...] = jnp.sum(received[...], axis=0)


def device_sum(keep, send):
    half = PACKED // 2
    other = lax.ppermute(send, AXES, SIBLING)
    copies = call(add_spread_kernel, "join", shape(16, half, 128), (keep, other), 10**6)
    received = lax.all_to_all(copies, AXES, 0, 0, axis_index_groups=PLANE)
    copies = call(sum_spread_kernel, "resum", shape(8, half, 128), (received,), 10**6)
    received = lax.all_to_all(copies, AXES, 0, 0, axis_index_groups=DEPTH)
    total = call(sum_kernel, "sum", shape(half, 128), (received,), 10**6)
    return total, lax.ppermute(total, AXES, SIBLING)


def dot(left, right, dims=(((1,), (0,)), ((), ()))):
    return lax.dot_general(left, right, dims, precision=highest, preferred_element_type=f32)


def finish_kernel(inside, own, other, *refs):
    powers, (solution_out, residual_out) = refs[:-2], refs[-2:]
    core = inside[4] > 0
    own, other = own[...], other[...]
    gram = unpack_gram(jnp.where(core, other, own), jnp.where(core, own, other))
    coefficients, update = small_solve(gram[:PANEL, :PANEL])
    row = lax.broadcasted_iota(jnp.int32, (BLOCK, PANEL), 0)
    column = lax.broadcasted_iota(jnp.int32, (BLOCK, PANEL), 1)
    identity = jnp.where(row == column, 1.0, 0.0)
    remainder = identity - update.T
    zeros = lambda width: [jnp.zeros((BLOCK, width), f32)] if width else []
    mixing = jnp.concatenate(
        [
            jnp.concatenate(
                zeros(BLOCK * j) + [remainder] + zeros(WIDTH - PANEL - BLOCK * j), axis=1
            )
            for j in range(STEPS + 1)
        ],
        axis=0,
    )
    power = lax.broadcasted_iota(jnp.int32, (PANEL, WIDTH), 1) // BLOCK
    for j in range(STEPS + 1, SPAN):
        mixing = jnp.where(power == j, mixing * GROWTH ** (STEPS - j), mixing)
    second_gram = dot(dot(mixing, gram), mixing, NT)
    second_coefficients, second_update = small_solve(second_gram)
    first_weights = jnp.concatenate([coefficients.T] + zeros(WIDTH - INNER), axis=1)
    second = jnp.concatenate(
        [
            jnp.concatenate([second_coefficients.T] + zeros(BLOCK), axis=1),
            identity - second_update.T,
        ],
        axis=0,
    )
    weights = dot(second, mixing)
    weights = jnp.concatenate([weights[:BLOCK] + first_weights, weights[BLOCK:]], axis=0)
    for e, panel in enumerate(element_panels(powers)):
        mixed = dot(weights, panel)
        solution_out[:, e // 2, e % 2, :] = mixed[:BLOCK]
        residual_out[:, e // 2, e % 2, :] = mixed[BLOCK:]


def on_device(forcing, diag_blocks, coupling):
    wall, stream = lax.axis_index("wall"), lax.axis_index("stream")
    inside = jnp.stack([wall > 0, wall < 7, stream > 0, stream < 31, wall % 2 > 0])
    inside = inside.astype(jnp.int32)
    faces = call(start_kernel, "start", FACES, (forcing,), 10**6)
    parts = prepare(diag_blocks, coupling)
    powers = [*faces[:2]]
    rows = []
    for step in range(2 * STEPS):
        scale = 1.0 if step < STEPS else GROWTH
        faces, row = advance(faces, powers, parts, inside, scale)
        powers += faces[:2]
        rows.append(row)
    keep, send = call(
        pack_kernel,
        "pack",
        [shape(PACKED // 2, 128)] * 2,
        (inside, *rows, *powers),
        10**7,
        in_specs=[SMEM] + [VMEM] * (len(rows) + len(powers)),
    )
    own, other = device_sum(keep, send)
    return call(
        finish_kernel,
        "finish",
        [shape(BLOCK, 2, 2, ROWS)] * 2,
        (inside, own, other, *powers),
        10**8,
        in_specs=[SMEM] + [VMEM] * (2 + len(powers)),
    )


def solution(mesh):
    return jax.shard_map(
        on_device,
        mesh=mesh,
        in_specs=(
            P(None, "wall", "stream", None),
            P("wall", "stream", None, None),
            P(None, "wall", "stream", None, None),
        ),
        out_specs=(P(None, "wall", "stream", None), P(None, "wall", "stream", None)),
        check_vma=False,
    )
```

```python
import functools

import jax
import jax.numpy as jnp
from jax import lax
from jax.experimental import pallas as pl
from jax.experimental.pallas import tpu as pltpu
from jax.sharding import PartitionSpec as P

ROWS = 320
BLOCK = 16
STEPS = 4
PANEL = 80
INNER = PANEL - BLOCK
SPAN = 2 * STEPS + 1
basis_shift = 1.5
basis_scale = 0.8

f32 = jnp.float32
bf16 = jnp.bfloat16
highest = lax.Precision.HIGHEST
AXES = ("wall", "stream")
NT = (((1,), (1,)), ((), ()))
VMEM = pl.BlockSpec(memory_space=pltpu.VMEM)


def groups_by(key):
    found = {}
    for wall in range(8):
        for stream in range(32):
            place = key(wall // 2, wall % 2, stream % 4, stream // 4)
            found.setdefault(place, []).append(wall * 32 + stream)
    return list(found.values())


PLANE = groups_by(lambda x, core, y, z: (core, z))
DEPTH = groups_by(lambda x, core, y, z: (core, x, y))


def partners(partner):
    pairs = []
    for wall in range(8):
        for stream in range(32):
            other_wall, other_stream = partner(wall, stream)
            pairs.append((wall * 32 + stream, other_wall % 8 * 32 + other_stream % 32))
    return pairs


SIBLING = partners(lambda w, s: (w ^ 1, s))
ACROSS = partners(lambda w, s: (w - 1 + 2 * (w % 2), s))
EVEN = partners(lambda w, s: (w, s ^ 1))
ODD = partners(lambda w, s: (w, s - 1 + 2 * (s % 2)))
WIDTH = SPAN * BLOCK
PACKED = 96
GROWTH = 2.0**-4


def call(kernel, name, out_shape, operands, flops):
    return pl.pallas_call(
        kernel,
        in_specs=[VMEM] * len(operands),
        out_specs=jax.tree.map(lambda _: VMEM, out_shape),
        out_shape=out_shape,
        compiler_params=pltpu.CompilerParams(vmem_limit_bytes=8 * 2**20),
        cost_estimate=pl.CostEstimate(flops=flops, bytes_accessed=2**20, transcendentals=0),
        name=name,
    )(*operands)


def shape(*dims, dtype=f32):
    return pltpu.VMEM(dims, dtype)


def split(value):
    high = value.astype(bf16)
    return high, (value - high.astype(f32)).astype(bf16)


def prepare_kernel(diag, coupling, local_high, local_low, far_high, far_low):
    element = pl.program_id(0)
    wall, stream = element // 2, element % 2
    row = lax.broadcasted_iota(jnp.int32, (ROWS, ROWS), 0)
    column = lax.broadcasted_iota(jnp.int32, (ROWS, ROWS), 1)

    def store(high, low, at, matrix):
        high_part, low_part = split(matrix * (1.0 / basis_scale))
        high[element, :, at * ROWS : (at + 1) * ROWS] = high_part
        low[element, :, at * ROWS : (at + 1) * ROWS] = low_part

    store(local_high, local_low, 0, diag[0, 0] - jnp.where(row == column, basis_shift, 0.0))
    store(local_high, local_low, 1, coupling[1 - wall, 0, 0])
    store(local_high, local_low, 2, coupling[3 - stream, 0, 0])
    store(far_high, far_low, 0, coupling[wall, 0, 0])
    store(far_high, far_low, 1, coupling[2 + stream, 0, 0])


def prepare(diag_blocks, coupling):
    return pl.pallas_call(
        prepare_kernel,
        grid=(4,),
        in_specs=[
            pl.BlockSpec((1, 1, ROWS, ROWS), lambda e: (e // 2, e % 2, 0, 0)),
            pl.BlockSpec((4, 1, 1, ROWS, ROWS), lambda e: (0, e // 2, e % 2, 0, 0)),
        ],
        out_specs=[VMEM] * 4,
        out_shape=[shape(4, ROWS, 3 * ROWS, dtype=bf16)] * 2
        + [shape(4, ROWS, 2 * ROWS, dtype=bf16)] * 2,
        compiler_params=pltpu.CompilerParams(vmem_limit_bytes=24 * 2**20),
        cost_estimate=pl.CostEstimate(flops=0, bytes_accessed=2**24, transcendentals=0),
        name="prepare",
    )(
        pltpu.with_memory_space_constraint(diag_blocks, pltpu.HBM),
        pltpu.with_memory_space_constraint(coupling, pltpu.HBM),
    )


def times(high, low, sources):
    highs, lows = zip(*[split(source) for source in sources])
    high_source = jnp.concatenate(highs, axis=1)
    both = jnp.concatenate([high_source, jnp.concatenate(lows, axis=1)], axis=0)
    first = lax.dot_general(both, high, NT, preferred_element_type=f32)
    second = lax.dot_general(high_source, low, NT, preferred_element_type=f32)
    return first[:BLOCK] + (first[BLOCK:] + second)


def gram_row(powers):
    panels = element_panels(powers)
    return sum(
        lax.dot_general(
            panel[-BLOCK:], panel, NT, precision=highest, preferred_element_type=f32
        )
        for panel in panels
    )


def local_kernel(high, low, *refs):
    powers, (partial, row) = refs[:-2], refs[-2:]
    field = powers[-1]
    for w in range(2):
        for s in range(2):
            sources = [field[w, s], field[1 - w, s], field[w, 1 - s]]
            partial[w, s] = times(high[2 * w + s], low[2 * w + s], sources)
    row[...] = gram_row(powers)


def select(flag, yes, no):
    return jnp.where(flag > 0, yes, no)


def emit(flags, values, power, to_sibling, to_across, to_even, to_odd):
    core, odd = flags[4:5], flags[5:6]
    for w in range(2):
        for s in range(2):
            power[w, s] = values[w][s]
    for i in range(2):
        to_sibling[i] = select(core, values[0][i], values[1][i])
        to_across[i] = select(core, values[1][i], values[0][i])
        to_even[i] = select(odd, values[i][0], values[i][1])
        to_odd[i] = select(odd, values[i][1], values[i][0])


def far_kernel(scale, flags, partial, sibling, across, even, odd, high, low, *outs):
    core, parity = flags[4:5], flags[5:6]
    values = []
    for w in range(2):
        line = []
        for s in range(2):
            if w == 0:
                wall = select(core, sibling[s], across[s])
            else:
                wall = select(core, across[s], sibling[s])
            if s == 0:
                stream = select(parity, even[w], odd[w])
            else:
                stream = select(parity, odd[w], even[w])
            sources = [
                select(flags[w : w + 1], wall, 0.0),
                select(flags[2 + s : 3 + s], stream, 0.0),
            ]
            value = partial[w, s] + times(high[2 * w + s], low[2 * w + s], sources)
            line.append(value if scale == 1.0 else value * scale)
        values.append(line)
    emit(flags, values, *outs)


def start_kernel(flags, forcing, *outs):
    emit(flags, [[forcing[:, w, s, :] for s in range(2)] for w in range(2)], *outs)


FIELD = [shape(2, 2, BLOCK, ROWS)] + [shape(2, BLOCK, ROWS)] * 4


def advance(field, powers, parts, flags, scale):
    _, to_sibling, to_across, to_even, to_odd = field
    odd = lax.ppermute(to_odd, AXES, ODD)
    even = lax.ppermute(to_even, AXES, EVEN)
    across = lax.ppermute(to_across, AXES, ACROSS)
    sibling = lax.ppermute(to_sibling, AXES, SIBLING)
    local_high, local_low, far_high, far_low = parts
    partial, row = call(
        local_kernel,
        "local",
        [shape(2, 2, BLOCK, ROWS), shape(BLOCK, BLOCK * len(powers))],
        (local_high, local_low, *powers),
        10**9,
    )
    field = call(
        functools.partial(far_kernel, scale),
        "far",
        FIELD,
        (flags, partial, sibling, across, even, odd, far_high, far_low),
        10**9,
    )
    return field, row


def pack_kernel(flags, *refs):
    rows, powers, (keep, send) = refs[: SPAN - 1], refs[SPAN - 1 : -2], refs[-2:]
    lines = [row[...] for row in rows] + [gram_row(powers)]
    last = lines[8]
    first_half = jnp.concatenate(
        [last[:, :128], lines[7], jnp.concatenate([lines[6], lines[0]], axis=1)], axis=0
    )
    second_half = jnp.concatenate(
        [
            jnp.concatenate([lines[5], lines[1]], axis=1),
            jnp.concatenate([lines[4], lines[2]], axis=1),
            jnp.concatenate([lines[3], last[:, 128:], jnp.zeros((BLOCK, 48), f32)], axis=1),
        ],
        axis=0,
    )
    core = flags[4:5, :128]
    keep[...] = select(core, second_half, first_half)
    send[...] = select(core, first_half, second_half)


def unpack_gram(first, second):
    lines = [
        first[32:48, 112:],
        second[:16, 96:],
        second[16:32, 80:],
        second[32:48, :64],
        second[16:32, :80],
        second[:16, :96],
        first[32:48, :112],
        first[16:32],
        jnp.concatenate([first[:16], second[32:48, 64:80]], axis=1),
    ]
    lower = jnp.concatenate(
        [
            line
            if line.shape[1] == WIDTH
            else jnp.concatenate([line, jnp.zeros((BLOCK, WIDTH - line.shape[1]), f32)], axis=1)
            for line in lines
        ],
        axis=0,
    )
    row = lax.broadcasted_iota(jnp.int32, (WIDTH, WIDTH), 0) // BLOCK
    column = lax.broadcasted_iota(jnp.int32, (WIDTH, WIDTH), 1) // BLOCK
    return jnp.where(row >= column, lower, lower.T)


def small_solve(gram):
    right = basis_shift * gram[:, :INNER] + basis_scale * gram[:, BLOCK:]
    normal = basis_shift * right[:INNER] + basis_scale * right[BLOCK:]
    target = basis_shift * gram[:INNER, :BLOCK] + basis_scale * gram[BLOCK:, :BLOCK]
    system = jnp.concatenate([normal, target, jnp.zeros((INNER, 48), f32)], axis=1)
    rows = lax.broadcasted_iota(jnp.int32, (INNER, 128), 0)
    group = 8
    for start in range(0, INNER, group):
        columns = [
            jnp.broadcast_to(system[:, start + j : start + j + 1], (INNER, 128))
            for j in range(group)
        ]
        for j in range(group):
            k = start + j
            inverse = 1.0 / columns[j][k : k + 1]
            pivot_row = system[k : k + 1] * inverse
            system = jnp.where(rows == k, pivot_row, system - columns[j] * pivot_row)
            for later in range(j + 1, group):
                scaled = columns[later][k : k + 1] * inverse
                columns[later] = jnp.where(
                    rows == k, scaled, columns[later] - columns[j] * scaled
                )
    coefficients = system[:, INNER:PANEL]
    zero = jnp.zeros((BLOCK, BLOCK), f32)
    update = basis_shift * jnp.concatenate([coefficients, zero], axis=0)
    update = update + basis_scale * jnp.concatenate([zero, coefficients], axis=0)
    return coefficients, update


def element_panels(powers):
    return [
        jnp.concatenate([power[w, s] for power in powers], axis=0)
        for w in range(2)
        for s in range(2)
    ]


def add_spread_kernel(own, other, copies):
    copies[...] = jnp.broadcast_to((own[...] + other[...])[None], copies.shape)


def sum_spread_kernel(received, copies):
    copies[...] = jnp.broadcast_to(jnp.sum(received[...], axis=0)[None], copies.shape)


def sum_kernel(received, total):
    total[...] = jnp.sum(received[...], axis=0)


def device_sum(keep, send):
    half = PACKED // 2
    other = lax.ppermute(send, AXES, SIBLING)
    copies = call(add_spread_kernel, "join", shape(16, half, 128), (keep, other), 10**6)
    received = lax.all_to_all(copies, AXES, 0, 0, axis_index_groups=PLANE)
    copies = call(sum_spread_kernel, "resum", shape(8, half, 128), (received,), 10**6)
    received = lax.all_to_all(copies, AXES, 0, 0, axis_index_groups=DEPTH)
    total = call(sum_kernel, "sum", shape(half, 128), (received,), 10**6)
    return total, lax.ppermute(total, AXES, SIBLING)


def dot(left, right, dims=(((1,), (0,)), ((), ()))):
    return lax.dot_general(left, right, dims, precision=highest, preferred_element_type=f32)


def finish_kernel(flags, own, other, *refs):
    powers, (solution_out, residual_out) = refs[:-2], refs[-2:]
    core = flags[4:5, :128]
    own, other = own[...], other[...]
    gram = unpack_gram(select(core, other, own), select(core, own, other))
    coefficients, update = small_solve(gram[:PANEL, :PANEL])
    row = lax.broadcasted_iota(jnp.int32, (BLOCK, PANEL), 0)
    column = lax.broadcasted_iota(jnp.int32, (BLOCK, PANEL), 1)
    identity = jnp.where(row == column, 1.0, 0.0)
    remainder = identity - update.T
    zeros = lambda width: [jnp.zeros((BLOCK, width), f32)] if width else []
    mixing = jnp.concatenate(
        [
            jnp.concatenate(
                zeros(BLOCK * j) + [remainder] + zeros(WIDTH - PANEL - BLOCK * j), axis=1
            )
            for j in range(STEPS + 1)
        ],
        axis=0,
    )
    power = lax.broadcasted_iota(jnp.int32, (PANEL, WIDTH), 1) // BLOCK
    for j in range(STEPS + 1, SPAN):
        mixing = jnp.where(power == j, mixing * GROWTH ** (STEPS - j), mixing)
    second_gram = dot(dot(mixing, gram), mixing, NT)
    second_coefficients, second_update = small_solve(second_gram)
    first_weights = jnp.concatenate([coefficients.T] + zeros(WIDTH - INNER), axis=1)
    second = jnp.concatenate(
        [
            jnp.concatenate([second_coefficients.T] + zeros(BLOCK), axis=1),
            identity - second_update.T,
        ],
        axis=0,
    )
    weights = dot(second, mixing)
    weights = jnp.concatenate([weights[:BLOCK] + first_weights, weights[BLOCK:]], axis=0)
    for e, panel in enumerate(element_panels(powers)):
        mixed = dot(weights, panel)
        solution_out[:, e // 2, e % 2, :] = mixed[:BLOCK]
        residual_out[:, e // 2, e % 2, :] = mixed[BLOCK:]


def on_device(forcing, diag_blocks, coupling):
    wall, stream = lax.axis_index("wall"), lax.axis_index("stream")
    flags = jnp.stack(
        [wall > 0, wall < 7, stream > 0, stream < 31, wall % 2 > 0, stream % 2 > 0, False, False]
    )
    flags = jnp.broadcast_to(flags.astype(f32)[:, None], (8, ROWS))
    field = call(start_kernel, "start", FIELD, (flags, forcing), 10**6)
    parts = prepare(diag_blocks, coupling)
    powers = [field[0]]
    rows = []
    for step in range(2 * STEPS):
        scale = 1.0 if step < STEPS else GROWTH
        field, row = advance(field, powers, parts, flags, scale)
        powers.append(field[0])
        rows.append(row)
    keep, send = call(
        pack_kernel, "pack", [shape(PACKED // 2, 128)] * 2, (flags, *rows, *powers), 10**7
    )
    own, other = device_sum(keep, send)
    return call(
        finish_kernel,
        "finish",
        [jax.ShapeDtypeStruct((BLOCK, 2, 2, ROWS), f32)] * 2,
        (flags, own, other, *powers),
        10**8,
    )


def solution(mesh):
    return jax.shard_map(
        on_device,
        mesh=mesh,
        in_specs=(
            P(None, "wall", "stream", None),
            P("wall", "stream", None, None),
            P(None, "wall", "stream", None, None),
        ),
        out_specs=(P(None, "wall", "stream", None), P(None, "wall", "stream", None)),
        check_vma=False,
    )
```

```python
import functools

import jax
import jax.numpy as jnp
from jax import lax
from jax.experimental import pallas as pl
from jax.experimental.pallas import tpu as pltpu
from jax.sharding import PartitionSpec as P

ROWS = 320
BLOCK = 16
STEPS = 4
PANEL = 80
INNER = PANEL - BLOCK
SPAN = 2 * STEPS + 1
basis_shift = 1.5
basis_scale = 0.8

f32 = jnp.float32
bf16 = jnp.bfloat16
highest = lax.Precision.HIGHEST
AXES = ("wall", "stream")
NT = (((1,), (1,)), ((), ()))
VMEM = pl.BlockSpec(memory_space=pltpu.VMEM)


def groups_by(key):
    found = {}
    for wall in range(8):
        for stream in range(32):
            place = key(wall // 2, wall % 2, stream % 4, stream // 4)
            found.setdefault(place, []).append(wall * 32 + stream)
    return list(found.values())


PLANE = groups_by(lambda x, core, y, z: (core, z))
DEPTH = groups_by(lambda x, core, y, z: (core, x, y))


def partners(partner):
    pairs = []
    for wall in range(8):
        for stream in range(32):
            other_wall, other_stream = partner(wall, stream)
            pairs.append((wall * 32 + stream, other_wall % 8 * 32 + other_stream % 32))
    return pairs


SIBLING = partners(lambda w, s: (w ^ 1, s))
ACROSS = partners(lambda w, s: (w - 1 + 2 * (w % 2), s))
EVEN = partners(lambda w, s: (w, s ^ 1))
ODD = partners(lambda w, s: (w, s - 1 + 2 * (s % 2)))
WIDTH = SPAN * BLOCK
PACKED = 96
GROWTH = 2.0**-4


def call(kernel, name, out_shape, operands, flops):
    return pl.pallas_call(
        kernel,
        in_specs=[VMEM] * len(operands),
        out_specs=jax.tree.map(lambda _: VMEM, out_shape),
        out_shape=out_shape,
        compiler_params=pltpu.CompilerParams(vmem_limit_bytes=8 * 2**20),
        cost_estimate=pl.CostEstimate(flops=flops, bytes_accessed=2**20, transcendentals=0),
        name=name,
    )(*operands)


def shape(*dims, dtype=f32):
    return pltpu.VMEM(dims, dtype)


def split(value):
    high = value.astype(bf16)
    return high, (value - high.astype(f32)).astype(bf16)


def prepare_kernel(diag, coupling, local_high, local_low, far_high, far_low):
    element = pl.program_id(0)
    wall, stream = element // 2, element % 2
    row = lax.broadcasted_iota(jnp.int32, (ROWS, ROWS), 0)
    column = lax.broadcasted_iota(jnp.int32, (ROWS, ROWS), 1)

    def store(high, low, at, matrix):
        high_part, low_part = split(matrix)
        high[element, :, at * ROWS : (at + 1) * ROWS] = high_part
        low[element, :, at * ROWS : (at + 1) * ROWS] = low_part

    store(local_high, local_low, 0, diag[0, 0] - jnp.where(row == column, basis_shift, 0.0))
    store(local_high, local_low, 1, coupling[1 - wall, 0, 0])
    store(local_high, local_low, 2, coupling[3 - stream, 0, 0])
    store(far_high, far_low, 0, coupling[wall, 0, 0])
    store(far_high, far_low, 1, coupling[2 + stream, 0, 0])


def prepare(diag_blocks, coupling):
    return pl.pallas_call(
        prepare_kernel,
        grid=(4,),
        in_specs=[
            pl.BlockSpec((1, 1, ROWS, ROWS), lambda e: (e // 2, e % 2, 0, 0)),
            pl.BlockSpec((4, 1, 1, ROWS, ROWS), lambda e: (0, e // 2, e % 2, 0, 0)),
        ],
        out_specs=[VMEM] * 4,
        out_shape=[shape(4, ROWS, 3 * ROWS, dtype=bf16)] * 2
        + [shape(4, ROWS, 2 * ROWS, dtype=bf16)] * 2,
        compiler_params=pltpu.CompilerParams(vmem_limit_bytes=24 * 2**20),
        cost_estimate=pl.CostEstimate(flops=0, bytes_accessed=2**24, transcendentals=0),
        name="prepare",
    )(
        pltpu.with_memory_space_constraint(diag_blocks, pltpu.HBM),
        pltpu.with_memory_space_constraint(coupling, pltpu.HBM),
    )


def times(high, low, sources):
    highs, lows = zip(*sources)
    high_source = jnp.concatenate(highs, axis=1)
    both = jnp.concatenate([high_source, jnp.concatenate(lows, axis=1)], axis=0)
    first = lax.dot_general(both, high, NT, preferred_element_type=f32)
    second = lax.dot_general(high_source, low, NT, preferred_element_type=f32)
    return first[:BLOCK] + (first[BLOCK:] + second)


def gram_row(powers):
    with_high, with_low = 0.0, 0.0
    for w in range(2):
        for s in range(2):
            last = jnp.concatenate([part[w, s] for part in powers[-1]], axis=0)
            highs = jnp.concatenate([high[w, s] for high, _ in powers], axis=0)
            lows = jnp.concatenate([low[w, s] for _, low in powers], axis=0)
            with_high += lax.dot_general(last, highs, NT, preferred_element_type=f32)
            with_low += lax.dot_general(last, lows, NT, preferred_element_type=f32)
    return with_high[:BLOCK] + (with_high[BLOCK:] + with_low[:BLOCK] + with_low[BLOCK:])


def pairs_of(refs):
    return list(zip(refs[::2], refs[1::2]))


def local_kernel(high, low, *refs):
    powers, (partial, row) = pairs_of(refs[:-2]), refs[-2:]
    field_high, field_low = powers[-1]
    for w in range(2):
        for s in range(2):
            places = [(w, s), (1 - w, s), (w, 1 - s)]
            sources = [(field_high[place], field_low[place]) for place in places]
            partial[w, s] = times(high[2 * w + s], low[2 * w + s], sources)
    row[...] = gram_row(powers)


def select(flag, yes, no):
    return jnp.where(flag > 0, yes, no)


def emit(flags, values, high, low, to_odd, to_even, to_across, to_sibling):
    core, odd = flags[4:5], flags[5:6]
    for i in range(2):
        to_odd[i] = select(odd, values[i][1], values[i][0])
        to_even[i] = select(odd, values[i][0], values[i][1])
        to_across[i] = select(core, values[1][i], values[0][i])
        to_sibling[i] = select(core, values[0][i], values[1][i])
    for w in range(2):
        for s in range(2):
            high[w, s], low[w, s] = split(values[w][s])


def next_power(scale, flags, partial, odd, even, across, sibling, high, low):
    core, parity = flags[4:5], flags[5:6]
    values = []
    for w in range(2):
        line = []
        for s in range(2):
            if w == 0:
                wall = select(core, sibling[s], across[s])
            else:
                wall = select(core, across[s], sibling[s])
            if s == 0:
                stream = select(parity, even[w], odd[w])
            else:
                stream = select(parity, odd[w], even[w])
            sources = [
                split(select(flags[w : w + 1], wall, 0.0)),
                split(select(flags[2 + s : 3 + s], stream, 0.0)),
            ]
            value = partial[w, s] + times(high[2 * w + s], low[2 * w + s], sources)
            line.append(value * (scale / basis_scale))
        values.append(line)
    return values


def far_kernel(scale, flags, partial, odd, even, across, sibling, high, low, *outs):
    emit(flags, next_power(scale, flags, partial, odd, even, across, sibling, high, low), *outs)


def last_kernel(scale, flags, partial, odd, even, across, sibling, high, low, *refs):
    rows, powers = refs[: SPAN - 1], pairs_of(refs[SPAN - 1 : -4])
    last_high, last_low, keep, send = refs[-4:]
    values = next_power(scale, flags, partial, odd, even, across, sibling, high, low)
    last = {}
    for w in range(2):
        for s in range(2):
            last[w, s] = split(values[w][s])
            last_high[w, s], last_low[w, s] = last[w, s]
    pair = tuple({place: parts[i] for place, parts in last.items()} for i in range(2))
    pack(flags, [row[...] for row in rows] + [gram_row(powers + [pair])], keep, send)


def start_kernel(flags, forcing, *outs):
    emit(flags, [[forcing[:, w, s, :] for s in range(2)] for w in range(2)], *outs)


FIELD = [shape(2, 2, BLOCK, ROWS, dtype=bf16)] * 2 + [shape(2, BLOCK, ROWS)] * 4


def exchange(faces):
    to_odd, to_even, to_across, to_sibling = faces
    sibling = lax.ppermute(to_sibling, AXES, SIBLING)
    across = lax.ppermute(to_across, AXES, ACROSS)
    even = lax.ppermute(to_even, AXES, EVEN)
    odd = lax.ppermute(to_odd, AXES, ODD)
    return odd, even, across, sibling


def pack(flags, lines, keep, send):
    last = lines[8]
    first_half = jnp.concatenate(
        [last[:, :128], lines[7], jnp.concatenate([lines[6], lines[0]], axis=1)], axis=0
    )
    second_half = jnp.concatenate(
        [
            jnp.concatenate([lines[5], lines[1]], axis=1),
            jnp.concatenate([lines[4], lines[2]], axis=1),
            jnp.concatenate([lines[3], last[:, 128:], jnp.zeros((BLOCK, 48), f32)], axis=1),
        ],
        axis=0,
    )
    core = flags[4:5, :128]
    keep[...] = select(core, second_half, first_half)
    send[...] = select(core, first_half, second_half)


def unpack_gram(first, second):
    lines = [
        first[32:48, 112:],
        second[:16, 96:],
        second[16:32, 80:],
        second[32:48, :64],
        second[16:32, :80],
        second[:16, :96],
        first[32:48, :112],
        first[16:32],
        jnp.concatenate([first[:16], second[32:48, 64:80]], axis=1),
    ]
    lower = jnp.concatenate(
        [
            line
            if line.shape[1] == WIDTH
            else jnp.concatenate([line, jnp.zeros((BLOCK, WIDTH - line.shape[1]), f32)], axis=1)
            for line in lines
        ],
        axis=0,
    )
    row = lax.broadcasted_iota(jnp.int32, (WIDTH, WIDTH), 0) // BLOCK
    column = lax.broadcasted_iota(jnp.int32, (WIDTH, WIDTH), 1) // BLOCK
    return jnp.where(row >= column, lower, lower.T)


def small_solve(gram):
    right = basis_shift * gram[:, :INNER] + basis_scale * gram[:, BLOCK:]
    normal = basis_shift * right[:INNER] + basis_scale * right[BLOCK:]
    target = basis_shift * gram[:INNER, :BLOCK] + basis_scale * gram[BLOCK:, :BLOCK]
    system = jnp.concatenate([normal, target, jnp.zeros((INNER, 48), f32)], axis=1)
    rows = lax.broadcasted_iota(jnp.int32, (INNER, 128), 0)
    group = 8
    for start in range(0, INNER, group):
        columns = [
            jnp.broadcast_to(system[:, start + j : start + j + 1], (INNER, 128))
            for j in range(group)
        ]
        for j in range(group):
            k = start + j
            inverse = 1.0 / columns[j][k : k + 1]
            pivot_row = system[k : k + 1] * inverse
            system = jnp.where(rows == k, pivot_row, system - columns[j] * pivot_row)
            for later in range(j + 1, group):
                scaled = columns[later][k : k + 1] * inverse
                columns[later] = jnp.where(
                    rows == k, scaled, columns[later] - columns[j] * scaled
                )
    coefficients = system[:, INNER:PANEL]
    zero = jnp.zeros((BLOCK, BLOCK), f32)
    update = basis_shift * jnp.concatenate([coefficients, zero], axis=0)
    update = update + basis_scale * jnp.concatenate([zero, coefficients], axis=0)
    return coefficients, update


def add_spread_kernel(own, other, copies):
    copies[...] = jnp.broadcast_to((own[...] + other[...])[None], copies.shape)


def sum_spread_kernel(received, copies):
    copies[...] = jnp.broadcast_to(jnp.sum(received[...], axis=0)[None], copies.shape)


def sum_kernel(received, total):
    total[...] = jnp.sum(received[...], axis=0)


def device_sum(keep, send):
    half = PACKED // 2
    other = lax.ppermute(send, AXES, SIBLING)
    copies = call(add_spread_kernel, "join", shape(16, half, 128), (keep, other), 10**6)
    received = lax.all_to_all(copies, AXES, 0, 0, axis_index_groups=PLANE)
    copies = call(sum_spread_kernel, "resum", shape(8, half, 128), (received,), 10**6)
    received = lax.all_to_all(copies, AXES, 0, 0, axis_index_groups=DEPTH)
    total = call(sum_kernel, "sum", shape(half, 128), (received,), 10**6)
    return total, lax.ppermute(total, AXES, SIBLING)


def dot(left, right, dims=(((1,), (0,)), ((), ()))):
    return lax.dot_general(left, right, dims, precision=highest, preferred_element_type=f32)


def finish_kernel(flags, own, other, *refs):
    powers, (solution_out, residual_out) = pairs_of(refs[:-2]), refs[-2:]
    core = flags[4:5, :128]
    own, other = own[...], other[...]
    gram = unpack_gram(select(core, other, own), select(core, own, other))
    coefficients, update = small_solve(gram[:PANEL, :PANEL])
    row = lax.broadcasted_iota(jnp.int32, (BLOCK, PANEL), 0)
    column = lax.broadcasted_iota(jnp.int32, (BLOCK, PANEL), 1)
    identity = jnp.where(row == column, 1.0, 0.0)
    remainder = identity - update.T
    zeros = lambda width: [jnp.zeros((BLOCK, width), f32)] if width else []
    mixing = jnp.concatenate(
        [
            jnp.concatenate(
                zeros(BLOCK * j) + [remainder] + zeros(WIDTH - PANEL - BLOCK * j), axis=1
            )
            for j in range(STEPS + 1)
        ],
        axis=0,
    )
    power = lax.broadcasted_iota(jnp.int32, (PANEL, WIDTH), 1) // BLOCK
    for j in range(STEPS + 1, SPAN):
        mixing = jnp.where(power == j, mixing * GROWTH ** (STEPS - j), mixing)
    second_gram = dot(dot(mixing, gram), mixing, NT)
    second_coefficients, second_update = small_solve(second_gram)
    first_weights = jnp.concatenate([coefficients.T] + zeros(WIDTH - INNER), axis=1)
    second = jnp.concatenate(
        [
            jnp.concatenate([second_coefficients.T] + zeros(BLOCK), axis=1),
            identity - second_update.T,
        ],
        axis=0,
    )
    weights = dot(second, mixing)
    weights = jnp.concatenate([weights[:BLOCK] + first_weights, weights[BLOCK:]], axis=0)
    first, rest = split(weights)
    third = (weights - first.astype(f32) - rest.astype(f32)).astype(bf16)
    parts = jnp.concatenate([first, rest, third], axis=0)
    count = 2 * BLOCK
    plain = (((1,), (0,)), ((), ()))
    for w in range(2):
        for s in range(2):
            highs = jnp.concatenate([high[w, s] for high, _ in powers], axis=0)
            lows = jnp.concatenate([low[w, s] for _, low in powers], axis=0)
            of_high = lax.dot_general(parts, highs, plain, preferred_element_type=f32)
            of_low = lax.dot_general(parts[: 2 * count], lows, plain, preferred_element_type=f32)
            small = of_high[count : 2 * count] + of_low[:count]
            small = small + (of_high[2 * count :] + of_low[count:])
            mixed = of_high[:count] + small
            solution_out[:, w, s, :] = mixed[:BLOCK]
            residual_out[:, w, s, :] = mixed[BLOCK:]


def on_device(forcing, diag_blocks, coupling):
    wall, stream = lax.axis_index("wall"), lax.axis_index("stream")
    flags = jnp.stack(
        [wall > 0, wall < 7, stream > 0, stream < 31, wall % 2 > 0, stream % 2 > 0, False, False]
    )
    flags = jnp.broadcast_to(flags.astype(f32)[:, None], (8, ROWS))
    field = call(start_kernel, "start", FIELD, (flags, forcing), 10**6)
    parts = prepare(diag_blocks, coupling)
    local_high, local_low, far_high, far_low = parts
    powers, rows = [*field[:2]], []
    for step in range(2 * STEPS):
        halo = exchange(field[2:])
        partial, row = call(
            local_kernel,
            "local",
            [shape(2, 2, BLOCK, ROWS), shape(BLOCK, BLOCK * (step + 1))],
            (local_high, local_low, *powers),
            10**9,
        )
        rows.append(row)
        scale = 1.0 if step < STEPS else GROWTH
        operands = (flags, partial, *halo, far_high, far_low)
        if step < 2 * STEPS - 1:
            kernel = functools.partial(far_kernel, scale)
            field = call(kernel, "far", FIELD, operands, 10**9)
            powers += field[:2]
    *last, keep, send = call(
        functools.partial(last_kernel, scale),
        "last",
        FIELD[:2] + [shape(PACKED // 2, 128)] * 2,
        (*operands, *rows, *powers),
        10**9,
    )
    powers += last
    own, other = device_sum(keep, send)
    return call(
        finish_kernel,
        "finish",
        [jax.ShapeDtypeStruct((BLOCK, 2, 2, ROWS), f32)] * 2,
        (flags, own, other, *powers),
        10**8,
    )


def solution(mesh):
    return jax.shard_map(
        on_device,
        mesh=mesh,
        in_specs=(
            P(None, "wall", "stream", None),
            P("wall", "stream", None, None),
            P(None, "wall", "stream", None, None),
        ),
        out_specs=(P(None, "wall", "stream", None), P(None, "wall", "stream", None)),
        check_vma=False,
    )
```

```python
import functools

import jax
import jax.numpy as jnp
from jax import lax
from jax.experimental import pallas as pl
from jax.experimental.pallas import tpu as pltpu
from jax.sharding import PartitionSpec as P

ROWS = 320
BLOCK = 16
STEPS = 4
PANEL = 80
INNER = PANEL - BLOCK
SPAN = 2 * STEPS + 1
basis_shift = 1.5
basis_scale = 0.8

f32 = jnp.float32
bf16 = jnp.bfloat16
highest = lax.Precision.HIGHEST
AXES = ("wall", "stream")
NT = (((1,), (1,)), ((), ()))
VMEM = pl.BlockSpec(memory_space=pltpu.VMEM)


def groups_by(key):
    found = {}
    for wall in range(8):
        for stream in range(32):
            place = key(wall // 2, wall % 2, stream % 4, stream // 4)
            found.setdefault(place, []).append(wall * 32 + stream)
    return list(found.values())


PLANE = groups_by(lambda x, core, y, z: (core, z))
DEPTH = groups_by(lambda x, core, y, z: (core, x, y))


def partners(partner):
    pairs = []
    for wall in range(8):
        for stream in range(32):
            other_wall, other_stream = partner(wall, stream)
            pairs.append((wall * 32 + stream, other_wall % 8 * 32 + other_stream % 32))
    return pairs


SIBLING = partners(lambda w, s: (w ^ 1, s))
ACROSS = partners(lambda w, s: (w - 1 + 2 * (w % 2), s))
EVEN = partners(lambda w, s: (w, s ^ 1))
ODD = partners(lambda w, s: (w, s - 1 + 2 * (s % 2)))
WIDTH = SPAN * BLOCK
PACKED = 96
GROWTH = 2.0**-4


def call(kernel, name, out_shape, operands, flops):
    return pl.pallas_call(
        kernel,
        in_specs=[VMEM] * len(operands),
        out_specs=jax.tree.map(lambda _: VMEM, out_shape),
        out_shape=out_shape,
        compiler_params=pltpu.CompilerParams(vmem_limit_bytes=8 * 2**20),
        cost_estimate=pl.CostEstimate(flops=flops, bytes_accessed=2**20, transcendentals=0),
        name=name,
    )(*operands)


def shape(*dims, dtype=f32):
    return pltpu.VMEM(dims, dtype)


def split(value):
    high = value.astype(bf16)
    return high, (value - high.astype(f32)).astype(bf16)


def prepare_kernel(diag, coupling, local_high, local_low, far_high, far_low, raw, arrived):
    row = lax.broadcasted_iota(jnp.int32, (ROWS, ROWS), 0)
    column = lax.broadcasted_iota(jnp.int32, (ROWS, ROWS), 1)
    shift = jnp.where(row == column, basis_shift, 0.0)

    def fetches(element):
        wall, stream = element // 2, element % 2
        blocks = [diag.at[wall, stream]]
        for face in (1 - wall, 3 - stream, wall, 2 + stream):
            blocks.append(coupling.at[face, wall, stream])
        slots = [5 * element + i for i in range(5)]
        return [
            pltpu.make_async_copy(block, raw.at[slot], arrived.at[slot])
            for block, slot in zip(blocks, slots)
        ]

    for element in range(4):
        for fetch in fetches(element):
            fetch.start()

    def convert(element, carry):
        for i, fetch in enumerate(fetches(element)):
            fetch.wait()
            block = raw[5 * element + i]
            high_part, low_part = split(block - shift if i == 0 else block)
            high, low, at = (local_high, local_low, i) if i < 3 else (far_high, far_low, i - 3)
            high[element, :, at * ROWS : (at + 1) * ROWS] = high_part
            low[element, :, at * ROWS : (at + 1) * ROWS] = low_part
        return carry

    lax.fori_loop(0, 4, convert, 0)


def prepare(diag_blocks, coupling):
    return pl.pallas_call(
        prepare_kernel,
        in_specs=[pl.BlockSpec(memory_space=pltpu.HBM)] * 2,
        out_specs=[VMEM] * 4,
        out_shape=[shape(4, ROWS, 3 * ROWS, dtype=bf16)] * 2
        + [shape(4, ROWS, 2 * ROWS, dtype=bf16)] * 2,
        scratch_shapes=[pltpu.VMEM((20, ROWS, ROWS), f32), pltpu.SemaphoreType.DMA((20,))],
        compiler_params=pltpu.CompilerParams(vmem_limit_bytes=24 * 2**20),
        cost_estimate=pl.CostEstimate(flops=0, bytes_accessed=2**24, transcendentals=0),
        name="prepare",
    )(
        pltpu.with_memory_space_constraint(diag_blocks, pltpu.HBM),
        pltpu.with_memory_space_constraint(coupling, pltpu.HBM),
    )


def times(high, low, sources):
    highs, lows = zip(*sources)
    high_source = jnp.concatenate(highs, axis=1)
    both = jnp.concatenate([high_source, jnp.concatenate(lows, axis=1)], axis=0)
    first = lax.dot_general(both, high, NT, preferred_element_type=f32)
    second = lax.dot_general(high_source, low, NT, preferred_element_type=f32)
    return first[:BLOCK] + (first[BLOCK:] + second)


def gram_row(powers):
    with_high, with_low = 0.0, 0.0
    for w in range(2):
        for s in range(2):
            last = jnp.concatenate([part[w, s] for part in powers[-1]], axis=0)
            highs = jnp.concatenate([high[w, s] for high, _ in powers], axis=0)
            lows = jnp.concatenate([low[w, s] for _, low in powers], axis=0)
            with_high += lax.dot_general(last, highs, NT, preferred_element_type=f32)
            with_low += lax.dot_general(last, lows, NT, preferred_element_type=f32)
    return with_high[:BLOCK] + (with_high[BLOCK:] + with_low[:BLOCK] + with_low[BLOCK:])


def pairs_of(refs):
    return list(zip(refs[::2], refs[1::2]))


def local_kernel(high, low, *refs):
    powers, (partial, row) = pairs_of(refs[:-2]), refs[-2:]
    field_high, field_low = powers[-1]
    for w in range(2):
        for s in range(2):
            places = [(w, s), (1 - w, s), (w, 1 - s)]
            sources = [(field_high[place], field_low[place]) for place in places]
            partial[w, s] = times(high[2 * w + s], low[2 * w + s], sources)
    row[...] = gram_row(powers)


def select(flag, yes, no):
    return jnp.where(flag > 0, yes, no)


def emit(flags, values, high, low, to_odd, to_even, to_across, to_sibling):
    core, odd = flags[4:5], flags[5:6]
    for i in range(2):
        to_odd[i] = select(odd, values[i][1], values[i][0])
        to_even[i] = select(odd, values[i][0], values[i][1])
        to_across[i] = select(core, values[1][i], values[0][i])
        to_sibling[i] = select(core, values[0][i], values[1][i])
    for w in range(2):
        for s in range(2):
            high[w, s], low[w, s] = split(values[w][s])


def next_power(scale, flags, partial, odd, even, across, sibling, high, low):
    core, parity = flags[4:5], flags[5:6]
    values = []
    for w in range(2):
        line = []
        for s in range(2):
            if w == 0:
                wall = select(core, sibling[s], across[s])
            else:
                wall = select(core, across[s], sibling[s])
            if s == 0:
                stream = select(parity, even[w], odd[w])
            else:
                stream = select(parity, odd[w], even[w])
            sources = [
                split(select(flags[w : w + 1], wall, 0.0)),
                split(select(flags[2 + s : 3 + s], stream, 0.0)),
            ]
            value = partial[w, s] + times(high[2 * w + s], low[2 * w + s], sources)
            line.append(value * (scale / basis_scale))
        values.append(line)
    return values


def far_kernel(scale, flags, partial, odd, even, across, sibling, high, low, *outs):
    emit(flags, next_power(scale, flags, partial, odd, even, across, sibling, high, low), *outs)


def last_kernel(scale, flags, partial, odd, even, across, sibling, high, low, *refs):
    rows, powers = refs[: SPAN - 1], pairs_of(refs[SPAN - 1 : -4])
    last_high, last_low, keep, send = refs[-4:]
    values = next_power(scale, flags, partial, odd, even, across, sibling, high, low)
    last = {}
    for w in range(2):
        for s in range(2):
            last[w, s] = split(values[w][s])
            last_high[w, s], last_low[w, s] = last[w, s]
    pair = tuple({place: parts[i] for place, parts in last.items()} for i in range(2))
    pack(flags, [row[...] for row in rows] + [gram_row(powers + [pair])], keep, send)


def start_kernel(flags, forcing, *outs):
    emit(flags, [[forcing[:, w, s, :] for s in range(2)] for w in range(2)], *outs)


FIELD = [shape(2, 2, BLOCK, ROWS, dtype=bf16)] * 2 + [shape(2, BLOCK, ROWS)] * 4


def exchange(faces):
    to_odd, to_even, to_across, to_sibling = faces
    sibling = lax.ppermute(to_sibling, AXES, SIBLING)
    across = lax.ppermute(to_across, AXES, ACROSS)
    even = lax.ppermute(to_even, AXES, EVEN)
    odd = lax.ppermute(to_odd, AXES, ODD)
    return odd, even, across, sibling


def pack(flags, lines, keep, send):
    last = lines[8]
    first_half = jnp.concatenate(
        [last[:, :128], lines[7], jnp.concatenate([lines[6], lines[0]], axis=1)], axis=0
    )
    second_half = jnp.concatenate(
        [
            jnp.concatenate([lines[5], lines[1]], axis=1),
            jnp.concatenate([lines[4], lines[2]], axis=1),
            jnp.concatenate([lines[3], last[:, 128:], jnp.zeros((BLOCK, 48), f32)], axis=1),
        ],
        axis=0,
    )
    core = flags[4:5, :128]
    keep[...] = select(core, second_half, first_half)
    send[...] = select(core, first_half, second_half)


def unpack_gram(first, second):
    lines = [
        first[32:48, 112:],
        second[:16, 96:],
        second[16:32, 80:],
        second[32:48, :64],
        second[16:32, :80],
        second[:16, :96],
        first[32:48, :112],
        first[16:32],
        jnp.concatenate([first[:16], second[32:48, 64:80]], axis=1),
    ]
    lower = jnp.concatenate(
        [
            line
            if line.shape[1] == WIDTH
            else jnp.concatenate([line, jnp.zeros((BLOCK, WIDTH - line.shape[1]), f32)], axis=1)
            for line in lines
        ],
        axis=0,
    )
    row = lax.broadcasted_iota(jnp.int32, (WIDTH, WIDTH), 0) // BLOCK
    column = lax.broadcasted_iota(jnp.int32, (WIDTH, WIDTH), 1) // BLOCK
    return jnp.where(row >= column, lower, lower.T)


def small_solve(gram):
    right = basis_shift * gram[:, :INNER] + basis_scale * gram[:, BLOCK:]
    normal = basis_shift * right[:INNER] + basis_scale * right[BLOCK:]
    target = basis_shift * gram[:INNER, :BLOCK] + basis_scale * gram[BLOCK:, :BLOCK]
    system = jnp.concatenate([normal, target, jnp.zeros((INNER, 48), f32)], axis=1)
    rows = lax.broadcasted_iota(jnp.int32, (INNER, 128), 0)
    group = 8
    for start in range(0, INNER, group):
        columns = [
            jnp.broadcast_to(system[:, start + j : start + j + 1], (INNER, 128))
            for j in range(group)
        ]
        for j in range(group):
            k = start + j
            inverse = 1.0 / columns[j][k : k + 1]
            pivot_row = system[k : k + 1] * inverse
            system = jnp.where(rows == k, pivot_row, system - columns[j] * pivot_row)
            for later in range(j + 1, group):
                scaled = columns[later][k : k + 1] * inverse
                columns[later] = jnp.where(
                    rows == k, scaled, columns[later] - columns[j] * scaled
                )
    coefficients = system[:, INNER:PANEL]
    zero = jnp.zeros((BLOCK, BLOCK), f32)
    update = basis_shift * jnp.concatenate([coefficients, zero], axis=0)
    update = update + basis_scale * jnp.concatenate([zero, coefficients], axis=0)
    return coefficients, update


def add_spread_kernel(own, other, copies):
    copies[...] = jnp.broadcast_to((own[...] + other[...])[None], copies.shape)


def sum_spread_kernel(received, copies):
    copies[...] = jnp.broadcast_to(jnp.sum(received[...], axis=0)[None], copies.shape)


def sum_kernel(received, total):
    total[...] = jnp.sum(received[...], axis=0)


def device_sum(keep, send):
    half = PACKED // 2
    other = lax.ppermute(send, AXES, SIBLING)
    copies = call(add_spread_kernel, "join", shape(16, half, 128), (keep, other), 10**6)
    received = lax.all_to_all(copies, AXES, 0, 0, axis_index_groups=PLANE)
    copies = call(sum_spread_kernel, "resum", shape(8, half, 128), (received,), 10**6)
    received = lax.all_to_all(copies, AXES, 0, 0, axis_index_groups=DEPTH)
    total = call(sum_kernel, "sum", shape(half, 128), (received,), 10**6)
    return total, lax.ppermute(total, AXES, SIBLING)


def dot(left, right, dims=(((1,), (0,)), ((), ()))):
    return lax.dot_general(left, right, dims, precision=highest, preferred_element_type=f32)


def finish_kernel(flags, own, other, *refs):
    powers, (solution_out, residual_out) = pairs_of(refs[:-2]), refs[-2:]
    core = flags[4:5, :128]
    own, other = own[...], other[...]
    gram = unpack_gram(select(core, other, own), select(core, own, other))
    coefficients, update = small_solve(gram[:PANEL, :PANEL])
    row = lax.broadcasted_iota(jnp.int32, (BLOCK, PANEL), 0)
    column = lax.broadcasted_iota(jnp.int32, (BLOCK, PANEL), 1)
    identity = jnp.where(row == column, 1.0, 0.0)
    remainder = identity - update.T
    zeros = lambda width: [jnp.zeros((BLOCK, width), f32)] if width else []
    mixing = jnp.concatenate(
        [
            jnp.concatenate(
                zeros(BLOCK * j) + [remainder] + zeros(WIDTH - PANEL - BLOCK * j), axis=1
            )
            for j in range(STEPS + 1)
        ],
        axis=0,
    )
    power = lax.broadcasted_iota(jnp.int32, (PANEL, WIDTH), 1) // BLOCK
    for j in range(STEPS + 1, SPAN):
        mixing = jnp.where(power == j, mixing * GROWTH ** (STEPS - j), mixing)
    second_gram = dot(dot(mixing, gram), mixing, NT)
    second_coefficients, second_update = small_solve(second_gram)
    first_weights = jnp.concatenate([coefficients.T] + zeros(WIDTH - INNER), axis=1)
    second = jnp.concatenate(
        [
            jnp.concatenate([second_coefficients.T] + zeros(BLOCK), axis=1),
            identity - second_update.T,
        ],
        axis=0,
    )
    weights = dot(second, mixing)
    weights = jnp.concatenate([weights[:BLOCK] + first_weights, weights[BLOCK:]], axis=0)
    first, rest = split(weights)
    third = (weights - first.astype(f32) - rest.astype(f32)).astype(bf16)
    parts = jnp.concatenate([first, rest, third], axis=0)
    count = 2 * BLOCK
    plain = (((1,), (0,)), ((), ()))
    for w in range(2):
        for s in range(2):
            highs = jnp.concatenate([high[w, s] for high, _ in powers], axis=0)
            lows = jnp.concatenate([low[w, s] for _, low in powers], axis=0)
            of_high = lax.dot_general(parts, highs, plain, preferred_element_type=f32)
            of_low = lax.dot_general(parts[: 2 * count], lows, plain, preferred_element_type=f32)
            small = of_high[count : 2 * count] + of_low[:count]
            small = small + (of_high[2 * count :] + of_low[count:])
            mixed = of_high[:count] + small
            solution_out[:, w, s, :] = mixed[:BLOCK]
            residual_out[:, w, s, :] = mixed[BLOCK:]


def on_device(forcing, diag_blocks, coupling):
    wall, stream = lax.axis_index("wall"), lax.axis_index("stream")
    flags = jnp.stack(
        [wall > 0, wall < 7, stream > 0, stream < 31, wall % 2 > 0, stream % 2 > 0, False, False]
    )
    flags = jnp.broadcast_to(flags.astype(f32)[:, None], (8, ROWS))
    field = call(start_kernel, "start", FIELD, (flags, forcing), 10**6)
    parts = prepare(diag_blocks, coupling)
    local_high, local_low, far_high, far_low = parts
    powers, rows = [*field[:2]], []
    for step in range(2 * STEPS):
        halo = exchange(field[2:])
        partial, row = call(
            local_kernel,
            "local",
            [shape(2, 2, BLOCK, ROWS), shape(BLOCK, BLOCK * (step + 1))],
            (local_high, local_low, *powers),
            10**9,
        )
        rows.append(row)
        scale = 1.0 if step < STEPS else GROWTH
        operands = (flags, partial, *halo, far_high, far_low)
        if step < 2 * STEPS - 1:
            kernel = functools.partial(far_kernel, scale)
            field = call(kernel, "far", FIELD, operands, 10**9)
            powers += field[:2]
    *last, keep, send = call(
        functools.partial(last_kernel, scale),
        "last",
        FIELD[:2] + [shape(PACKED // 2, 128)] * 2,
        (*operands, *rows, *powers),
        10**9,
    )
    powers += last
    own, other = device_sum(keep, send)
    return call(
        finish_kernel,
        "finish",
        [jax.ShapeDtypeStruct((BLOCK, 2, 2, ROWS), f32)] * 2,
        (flags, own, other, *powers),
        10**8,
    )


def solution(mesh):
    return jax.shard_map(
        on_device,
        mesh=mesh,
        in_specs=(
            P(None, "wall", "stream", None),
            P("wall", "stream", None, None),
            P(None, "wall", "stream", None, None),
        ),
        out_specs=(P(None, "wall", "stream", None), P(None, "wall", "stream", None)),
        check_vma=False,
    )
```

```python
import functools

import jax
import jax.numpy as jnp
from jax import lax
from jax.experimental import pallas as pl
from jax.experimental.pallas import tpu as pltpu
from jax.sharding import PartitionSpec as P

ROWS = 320
BLOCK = 16
STEPS = 4
PANEL = 80
INNER = PANEL - BLOCK
SPAN = 2 * STEPS + 1
basis_shift = 1.5
basis_scale = 0.8

f32 = jnp.float32
bf16 = jnp.bfloat16
highest = lax.Precision.HIGHEST
AXES = ("wall", "stream")
NT = (((1,), (1,)), ((), ()))
VMEM = pl.BlockSpec(memory_space=pltpu.VMEM)


def groups_by(key):
    found = {}
    for wall in range(8):
        for stream in range(32):
            place = key(wall // 2, wall % 2, stream % 4, stream // 4)
            found.setdefault(place, []).append(wall * 32 + stream)
    return list(found.values())


PLANE = groups_by(lambda x, core, y, z: (core, z))
DEPTH = groups_by(lambda x, core, y, z: (core, x, y))


def partners(partner):
    pairs = []
    for wall in range(8):
        for stream in range(32):
            other_wall, other_stream = partner(wall, stream)
            pairs.append((wall * 32 + stream, other_wall % 8 * 32 + other_stream % 32))
    return pairs


SIBLING = partners(lambda w, s: (w ^ 1, s))
ACROSS = partners(lambda w, s: (w - 1 + 2 * (w % 2), s))
EVEN = partners(lambda w, s: (w, s ^ 1))
ODD = partners(lambda w, s: (w, s - 1 + 2 * (s % 2)))
WIDTH = SPAN * BLOCK
PACKED = 96
GROWTH = 2.0**-4


def call(kernel, name, out_shape, operands, flops):
    return pl.pallas_call(
        kernel,
        in_specs=[VMEM] * len(operands),
        out_specs=jax.tree.map(lambda _: VMEM, out_shape),
        out_shape=out_shape,
        compiler_params=pltpu.CompilerParams(vmem_limit_bytes=8 * 2**20),
        cost_estimate=pl.CostEstimate(flops=flops, bytes_accessed=2**20, transcendentals=0),
        name=name,
    )(*operands)


def shape(*dims, dtype=f32):
    return pltpu.VMEM(dims, dtype)


def split(value):
    high = value.astype(bf16)
    return high, (value - high.astype(f32)).astype(bf16)


def place(i, k):
    core, parity = lax.axis_index("wall") % 2, lax.axis_index("stream") % 2
    return (1 - core if i else core), (1 - parity if k else parity)


def prepare_kernel(diag, coupling, *refs):
    outs, (raw, arrived) = refs[:8], refs[8:]
    row = lax.broadcasted_iota(jnp.int32, (ROWS, ROWS), 0)
    column = lax.broadcasted_iota(jnp.int32, (ROWS, ROWS), 1)
    shift = jnp.where(row == column, basis_shift, 0.0)
    fetches, targets = [], []
    for i in range(2):
        for k in range(2):
            wall, stream = place(i, k)
            blocks = [diag.at[wall, stream]]
            for face in (1 - wall, 3 - stream, wall, 2 + stream):
                blocks.append(coupling.at[face, wall, stream])
            for block in blocks:
                slot = len(fetches)
                fetches.append(pltpu.make_async_copy(block, raw.at[slot], arrived.at[slot]))
            targets += [(0, 2 * i + k, at) for at in range(3)]
            targets += [(2, i, 0), (2, i, 1)] if k else [(4, i, 0), (6, i, 0)]
    for fetch in fetches:
        fetch.start()
    for slot, (out, index, at) in enumerate(targets):
        fetches[slot].wait()
        block = raw[slot]
        high_part, low_part = split(block - shift if slot % 5 == 0 else block)
        outs[out][index, :, at * ROWS : (at + 1) * ROWS] = high_part
        outs[out + 1][index, :, at * ROWS : (at + 1) * ROWS] = low_part


def prepare(diag_blocks, coupling):
    sizes = [(4, 3), (2, 2), (2, 1), (2, 1)]
    parts = pl.pallas_call(
        prepare_kernel,
        in_specs=[pl.BlockSpec(memory_space=pltpu.HBM)] * 2,
        out_specs=[VMEM] * 8,
        out_shape=[shape(n, ROWS, m * ROWS, dtype=bf16) for n, m in sizes for _ in range(2)],
        scratch_shapes=[pltpu.VMEM((20, ROWS, ROWS), f32), pltpu.SemaphoreType.DMA((20,))],
        compiler_params=pltpu.CompilerParams(vmem_limit_bytes=24 * 2**20),
        cost_estimate=pl.CostEstimate(flops=0, bytes_accessed=2**24, transcendentals=0),
        name="prepare",
    )(
        pltpu.with_memory_space_constraint(diag_blocks, pltpu.HBM),
        pltpu.with_memory_space_constraint(coupling, pltpu.HBM),
    )
    return parts[0:2], parts[2:4], parts[4:6], parts[6:8]


def times(high, low, sources):
    highs, lows = zip(*sources)
    high_source = jnp.concatenate(highs, axis=1)
    both = jnp.concatenate([high_source, jnp.concatenate(lows, axis=1)], axis=0)
    first = lax.dot_general(both, high, NT, preferred_element_type=f32)
    second = lax.dot_general(high_source, low, NT, preferred_element_type=f32)
    return first[:BLOCK] + (first[BLOCK:] + second)


def part(power, i, k):
    return power[2 * k][i], power[2 * k + 1][i]


def stacked(powers, i, k):
    highs, lows = zip(*[part(power, i, k) for power in powers])
    return jnp.concatenate(highs, axis=0), jnp.concatenate(lows, axis=0)


def gram_row(powers):
    with_high, with_low = 0.0, 0.0
    for i in range(2):
        for k in range(2):
            last = jnp.concatenate(part(powers[-1], i, k), axis=0)
            highs, lows = stacked(powers, i, k)
            with_high += lax.dot_general(last, highs, NT, preferred_element_type=f32)
            with_low += lax.dot_general(last, lows, NT, preferred_element_type=f32)
    return with_high[:BLOCK] + (with_high[BLOCK:] + with_low[:BLOCK] + with_low[BLOCK:])


def powers_of(refs):
    return [refs[at : at + 4] for at in range(0, len(refs), 4)]


def local_kernel(high, low, *refs):
    powers, (partial, row) = powers_of(refs[:-2]), refs[-2:]
    for i in range(2):
        for k in range(2):
            sources = [part(powers[-1], *at) for at in ((i, k), (1 - i, k), (i, 1 - k))]
            partial[i, k] = times(high[2 * i + k], low[2 * i + k], sources)
    row[...] = gram_row(powers)


def select(flag, yes, no):
    return jnp.where(flag > 0, yes, no)


def near_kernel(scale, flags, partial, even, across, sibling, *refs):
    even_high, even_low, wall_high, wall_low, high, low, to_even, odd_partial = refs
    inside = flags[0:1]
    for i in range(2):
        walls = [sibling[k] if i else select(inside, across[k], 0.0) for k in range(2)]
        sources = [split(walls[1]), split(even[i])]
        value = partial[i, 1] + times(even_high[i], even_low[i], sources)
        value = value * (scale / basis_scale)
        to_even[i] = value
        high[i], low[i] = split(value)
        odd_partial[i] = partial[i, 0] + times(wall_high[i], wall_low[i], [split(walls[0])])


def odd_side(scale, flags, odd, odd_partial, odd_high, odd_low):
    inside = flags[1:2]
    for i in range(2):
        sources = [split(select(inside, odd[i], 0.0))]
        value = odd_partial[i] + times(odd_high[i], odd_low[i], sources)
        yield i, value * (scale / basis_scale)


def odd_kernel(scale, flags, odd, odd_partial, even_side, odd_high, odd_low, *outs):
    high, low, to_odd, to_across, to_sibling = outs
    for i, value in odd_side(scale, flags, odd, odd_partial, odd_high, odd_low):
        to_odd[i] = value
        to_wall = to_sibling if i else to_across
        to_wall[0], to_wall[1] = value, even_side[i]
        high[i], low[i] = split(value)


def last_kernel(scale, flags, odd, odd_partial, odd_high, odd_low, *refs):
    outs, refs = refs[-4:], refs[:-4]
    rows, powers = refs[: SPAN - 1], powers_of(refs[SPAN - 1 : -2])
    last_high, last_low, keep, send = outs
    highs, lows = [], []
    for i, value in odd_side(scale, flags, odd, odd_partial, odd_high, odd_low):
        high_part, low_part = split(value)
        last_high[i], last_low[i] = high_part, low_part
        highs.append(high_part)
        lows.append(low_part)
    powers.append((highs, lows, *refs[-2:]))
    pack(flags, [row[...] for row in rows] + [gram_row(powers)], keep, send)


def start_kernel(flags, forcing, *outs):
    high0, low0, high1, low1, to_odd, to_even, to_across, to_sibling = outs
    core, parity = flags[4:5], flags[5:6]
    field = [[forcing[:, w, s, :] for s in range(2)] for w in range(2)]
    field = turned(core, parity, field)
    for i in range(2):
        to_odd[i], to_even[i] = field[i][0], field[i][1]
        to_wall = to_sibling if i else to_across
        to_wall[0], to_wall[1] = field[i][0], field[i][1]
        high0[i], low0[i] = split(field[i][0])
        high1[i], low1[i] = split(field[i][1])


def turned(core, parity, field):
    field = [[select(core, field[1 - i][k], field[i][k]) for k in range(2)] for i in range(2)]
    return [[select(parity, line[1 - k], line[k]) for k in range(2)] for line in field]


PAIR = [shape(2, BLOCK, ROWS, dtype=bf16)] * 2
FACE = shape(2, BLOCK, ROWS)


def pack(flags, lines, keep, send):
    last = lines[8]
    first_half = jnp.concatenate(
        [last[:, :128], lines[7], jnp.concatenate([lines[6], lines[0]], axis=1)], axis=0
    )
    second_half = jnp.concatenate(
        [
            jnp.concatenate([lines[5], lines[1]], axis=1),
            jnp.concatenate([lines[4], lines[2]], axis=1),
            jnp.concatenate([lines[3], last[:, 128:], jnp.zeros((BLOCK, 48), f32)], axis=1),
        ],
        axis=0,
    )
    core = flags[4:5, :128]
    keep[...] = select(core, second_half, first_half)
    send[...] = select(core, first_half, second_half)


def unpack_gram(first, second):
    lines = [
        first[32:48, 112:],
        second[:16, 96:],
        second[16:32, 80:],
        second[32:48, :64],
        second[16:32, :80],
        second[:16, :96],
        first[32:48, :112],
        first[16:32],
        jnp.concatenate([first[:16], second[32:48, 64:80]], axis=1),
    ]
    lower = jnp.concatenate(
        [
            line
            if line.shape[1] == WIDTH
            else jnp.concatenate([line, jnp.zeros((BLOCK, WIDTH - line.shape[1]), f32)], axis=1)
            for line in lines
        ],
        axis=0,
    )
    row = lax.broadcasted_iota(jnp.int32, (WIDTH, WIDTH), 0) // BLOCK
    column = lax.broadcasted_iota(jnp.int32, (WIDTH, WIDTH), 1) // BLOCK
    return jnp.where(row >= column, lower, lower.T)


def small_solve(gram):
    right = basis_shift * gram[:, :INNER] + basis_scale * gram[:, BLOCK:]
    normal = basis_shift * right[:INNER] + basis_scale * right[BLOCK:]
    target = basis_shift * gram[:INNER, :BLOCK] + basis_scale * gram[BLOCK:, :BLOCK]
    system = jnp.concatenate([normal, target, jnp.zeros((INNER, 48), f32)], axis=1)
    rows = lax.broadcasted_iota(jnp.int32, (INNER, 128), 0)
    group = 8
    for start in range(0, INNER, group):
        columns = [
            jnp.broadcast_to(system[:, start + j : start + j + 1], (INNER, 128))
            for j in range(group)
        ]
        for j in range(group):
            k = start + j
            inverse = 1.0 / columns[j][k : k + 1]
            pivot_row = system[k : k + 1] * inverse
            system = jnp.where(rows == k, pivot_row, system - columns[j] * pivot_row)
            for later in range(j + 1, group):
                scaled = columns[later][k : k + 1] * inverse
                columns[later] = jnp.where(
                    rows == k, scaled, columns[later] - columns[j] * scaled
                )
    coefficients = system[:, INNER:PANEL]
    zero = jnp.zeros((BLOCK, BLOCK), f32)
    update = basis_shift * jnp.concatenate([coefficients, zero], axis=0)
    update = update + basis_scale * jnp.concatenate([zero, coefficients], axis=0)
    return coefficients, update


def add_spread_kernel(own, other, copies):
    copies[...] = jnp.broadcast_to((own[...] + other[...])[None], copies.shape)


def sum_spread_kernel(received, copies):
    copies[...] = jnp.broadcast_to(jnp.sum(received[...], axis=0)[None], copies.shape)


def sum_kernel(received, total):
    total[...] = jnp.sum(received[...], axis=0)


def device_sum(keep, send):
    half = PACKED // 2
    other = lax.ppermute(send, AXES, SIBLING)
    copies = call(add_spread_kernel, "join", shape(16, half, 128), (keep, other), 10**6)
    received = lax.all_to_all(copies, AXES, 0, 0, axis_index_groups=PLANE)
    copies = call(sum_spread_kernel, "resum", shape(8, half, 128), (received,), 10**6)
    received = lax.all_to_all(copies, AXES, 0, 0, axis_index_groups=DEPTH)
    total = call(sum_kernel, "sum", shape(half, 128), (received,), 10**6)
    return total, lax.ppermute(total, AXES, SIBLING)


def dot(left, right, dims=(((1,), (0,)), ((), ()))):
    return lax.dot_general(left, right, dims, precision=highest, preferred_element_type=f32)


def finish_kernel(flags, own, other, *refs):
    powers, (solution_out, residual_out) = powers_of(refs[:-2]), refs[-2:]
    core = flags[4:5, :128]
    own, other = own[...], other[...]
    gram = unpack_gram(select(core, other, own), select(core, own, other))
    coefficients, update = small_solve(gram[:PANEL, :PANEL])
    row = lax.broadcasted_iota(jnp.int32, (BLOCK, PANEL), 0)
    column = lax.broadcasted_iota(jnp.int32, (BLOCK, PANEL), 1)
    identity = jnp.where(row == column, 1.0, 0.0)
    remainder = identity - update.T
    zeros = lambda width: [jnp.zeros((BLOCK, width), f32)] if width else []
    mixing = jnp.concatenate(
        [
            jnp.concatenate(
                zeros(BLOCK * j) + [remainder] + zeros(WIDTH - PANEL - BLOCK * j), axis=1
            )
            for j in range(STEPS + 1)
        ],
        axis=0,
    )
    power = lax.broadcasted_iota(jnp.int32, (PANEL, WIDTH), 1) // BLOCK
    for j in range(STEPS + 1, SPAN):
        mixing = jnp.where(power == j, mixing * GROWTH ** (STEPS - j), mixing)
    second_gram = dot(dot(mixing, gram), mixing, NT)
    second_coefficients, second_update = small_solve(second_gram)
    first_weights = jnp.concatenate([coefficients.T] + zeros(WIDTH - INNER), axis=1)
    second = jnp.concatenate(
        [
            jnp.concatenate([second_coefficients.T] + zeros(BLOCK), axis=1),
            identity - second_update.T,
        ],
        axis=0,
    )
    weights = dot(second, mixing)
    weights = jnp.concatenate([weights[:BLOCK] + first_weights, weights[BLOCK:]], axis=0)
    first, rest = split(weights)
    third = (weights - first.astype(f32) - rest.astype(f32)).astype(bf16)
    parts = jnp.concatenate([first, rest, third], axis=0)
    count = 2 * BLOCK
    plain = (((1,), (0,)), ((), ()))
    mixed = [[None, None], [None, None]]
    for i in range(2):
        for k in range(2):
            highs, lows = stacked(powers, i, k)
            of_high = lax.dot_general(parts, highs, plain, preferred_element_type=f32)
            of_low = lax.dot_general(parts[: 2 * count], lows, plain, preferred_element_type=f32)
            small = of_high[count : 2 * count] + of_low[:count]
            small = small + (of_high[2 * count :] + of_low[count:])
            mixed[i][k] = of_high[:count] + small
    mixed = turned(flags[4:5], flags[5:6], mixed)
    for w in range(2):
        for s in range(2):
            solution_out[:, w, s, :] = mixed[w][s][:BLOCK]
            residual_out[:, w, s, :] = mixed[w][s][BLOCK:]


def on_device(forcing, diag_blocks, coupling):
    wall, stream = lax.axis_index("wall"), lax.axis_index("stream")
    core, parity = wall % 2 > 0, stream % 2 > 0
    across_inside = jnp.where(core, wall < 7, wall > 0)
    odd_inside = jnp.where(parity, stream < 31, stream > 0)
    flags = jnp.stack([across_inside, odd_inside, False, False, core, parity, False, False])
    flags = jnp.broadcast_to(flags.astype(f32)[:, None], (8, ROWS))
    *field, to_odd, to_even, to_across, to_sibling = call(
        start_kernel, "start", PAIR * 2 + [FACE] * 4, (flags, forcing), 10**6
    )
    own_parts, even_parts, wall_parts, odd_parts = prepare(diag_blocks, coupling)
    powers, rows = [*field], []
    for step in range(2 * STEPS):
        odd = lax.ppermute(to_odd, AXES, ODD)
        even = lax.ppermute(to_even, AXES, EVEN)
        across = lax.ppermute(to_across, AXES, ACROSS)
        sibling = lax.ppermute(to_sibling, AXES, SIBLING)
        partial, row = call(
            local_kernel,
            "local",
            [shape(2, 2, BLOCK, ROWS), shape(BLOCK, BLOCK * (step + 1))],
            (*own_parts, *powers),
            10**9,
        )
        rows.append(row)
        scale = 1.0 if step < STEPS else GROWTH
        *even_side, to_even, odd_partial = call(
            functools.partial(near_kernel, scale),
            "near",
            PAIR + [FACE] * 2,
            (flags, partial, even, across, sibling, *even_parts, *wall_parts),
            10**9,
        )
        if step < 2 * STEPS - 1:
            *odd_side, to_odd, to_across, to_sibling = call(
                functools.partial(odd_kernel, scale),
                "odd",
                PAIR + [FACE] * 3,
                (flags, odd, odd_partial, to_even, *odd_parts),
                10**9,
            )
            powers += odd_side + even_side
    *odd_side, keep, send = call(
        functools.partial(last_kernel, scale),
        "last",
        PAIR + [shape(PACKED // 2, 128)] * 2,
        (flags, odd, odd_partial, *odd_parts, *rows, *powers, *even_side),
        10**9,
    )
    powers += odd_side + even_side
    own, other = device_sum(keep, send)
    return call(
        finish_kernel,
        "finish",
        [jax.ShapeDtypeStruct((BLOCK, 2, 2, ROWS), f32)] * 2,
        (flags, own, other, *powers),
        10**8,
    )


def solution(mesh):
    return jax.shard_map(
        on_device,
        mesh=mesh,
        in_specs=(
            P(None, "wall", "stream", None),
            P("wall", "stream", None, None),
            P(None, "wall", "stream", None, None),
        ),
        out_specs=(P(None, "wall", "stream", None), P(None, "wall", "stream", None)),
        check_vma=False,
    )
```

```python
import functools

import jax
import jax.numpy as jnp
from jax import lax
from jax.experimental import pallas as pl
from jax.experimental.pallas import tpu as pltpu
from jax.sharding import PartitionSpec as P

ROWS = 320
BLOCK = 16
STEPS = 4
PANEL = 80
INNER = PANEL - BLOCK
SPAN = 2 * STEPS + 1
basis_shift = 1.5
basis_scale = 0.8

f32 = jnp.float32
bf16 = jnp.bfloat16
highest = lax.Precision.HIGHEST
AXES = ("wall", "stream")
NT = (((1,), (1,)), ((), ()))
VMEM = pl.BlockSpec(memory_space=pltpu.VMEM)


def groups_by(key):
    found = {}
    for wall in range(8):
        for stream in range(32):
            place = key(wall // 2, wall % 2, stream % 4, stream // 4)
            found.setdefault(place, []).append(wall * 32 + stream)
    return list(found.values())


PLANE = groups_by(lambda x, core, y, z: (core, z))
DEPTH = groups_by(lambda x, core, y, z: (core, x, y))


def partners(partner):
    pairs = []
    for wall in range(8):
        for stream in range(32):
            other_wall, other_stream = partner(wall, stream)
            pairs.append((wall * 32 + stream, other_wall % 8 * 32 + other_stream % 32))
    return pairs


SIBLING = partners(lambda w, s: (w ^ 1, s))
ACROSS = partners(lambda w, s: (w - 1 + 2 * (w % 2), s))
EVEN = partners(lambda w, s: (w, s ^ 1))
ODD = partners(lambda w, s: (w, s - 1 + 2 * (s % 2)))
WIDTH = SPAN * BLOCK
PACKED = 96
GROWTH = 2.0**-4


def call(kernel, name, out_shape, operands, flops):
    return pl.pallas_call(
        kernel,
        in_specs=[VMEM] * len(operands),
        out_specs=jax.tree.map(lambda _: VMEM, out_shape),
        out_shape=out_shape,
        compiler_params=pltpu.CompilerParams(vmem_limit_bytes=8 * 2**20),
        cost_estimate=pl.CostEstimate(flops=flops, bytes_accessed=2**20, transcendentals=0),
        name=name,
    )(*operands)


def shape(*dims, dtype=f32):
    return pltpu.VMEM(dims, dtype)


def split(value):
    high = value.astype(bf16)
    return high, (value - high.astype(f32)).astype(bf16)


def place(i, k):
    core, parity = lax.axis_index("wall") % 2, lax.axis_index("stream") % 2
    return (1 - core if i else core), (1 - parity if k else parity)


def prepare_kernel(diag, coupling, *refs):
    outs, (raw, arrived) = refs[:8], refs[8:]
    row = lax.broadcasted_iota(jnp.int32, (ROWS, ROWS), 0)
    column = lax.broadcasted_iota(jnp.int32, (ROWS, ROWS), 1)
    shift = jnp.where(row == column, basis_shift, 0.0)
    fetches, targets = [], []
    for i in range(2):
        for k in range(2):
            wall, stream = place(i, k)
            blocks = [diag.at[wall, stream]]
            for face in (1 - wall, 3 - stream, wall, 2 + stream):
                blocks.append(coupling.at[face, wall, stream])
            for block in blocks:
                slot = len(fetches)
                fetches.append(pltpu.make_async_copy(block, raw.at[slot], arrived.at[slot]))
            targets += [(0, 2 * i + k, at) for at in range(3)]
            if i == k:
                targets += [(2, i, 0), (2, i, 1)]
            else:
                targets += [(6, 0, 0), (4, 0, 0)] if k else [(4, 1, 0), (6, 1, 0)]
    for fetch in fetches:
        fetch.start()
    for slot, (out, index, at) in enumerate(targets):
        fetches[slot].wait()
        block = raw[slot]
        high_part, low_part = split(block - shift if slot % 5 == 0 else block)
        outs[out][index, :, at * ROWS : (at + 1) * ROWS] = high_part
        outs[out + 1][index, :, at * ROWS : (at + 1) * ROWS] = low_part


def prepare(diag_blocks, coupling):
    sizes = [(4, 3), (2, 2), (2, 1), (2, 1)]
    parts = pl.pallas_call(
        prepare_kernel,
        in_specs=[pl.BlockSpec(memory_space=pltpu.HBM)] * 2,
        out_specs=[VMEM] * 8,
        out_shape=[shape(n, ROWS, m * ROWS, dtype=bf16) for n, m in sizes for _ in range(2)],
        scratch_shapes=[pltpu.VMEM((20, ROWS, ROWS), f32), pltpu.SemaphoreType.DMA((20,))],
        compiler_params=pltpu.CompilerParams(vmem_limit_bytes=24 * 2**20),
        cost_estimate=pl.CostEstimate(flops=0, bytes_accessed=2**24, transcendentals=0),
        name="prepare",
    )(
        pltpu.with_memory_space_constraint(diag_blocks, pltpu.HBM),
        pltpu.with_memory_space_constraint(coupling, pltpu.HBM),
    )
    return parts[0:2], parts[2:4], parts[4:6], parts[6:8]


def times(high, low, sources):
    highs, lows = zip(*sources)
    high_source = jnp.concatenate(highs, axis=1)
    both = jnp.concatenate([high_source, jnp.concatenate(lows, axis=1)], axis=0)
    first = lax.dot_general(both, high, NT, preferred_element_type=f32)
    second = lax.dot_general(high_source, low, NT, preferred_element_type=f32)
    return first[:BLOCK] + (first[BLOCK:] + second)


def part(power, i, k):
    return power[0][i, k], power[1][i, k]


def stacked(powers, i, k):
    highs, lows = zip(*[part(power, i, k) for power in powers])
    return jnp.concatenate(highs, axis=0), jnp.concatenate(lows, axis=0)


def gram_row(powers):
    with_high, with_low = 0.0, 0.0
    for i in range(2):
        for k in range(2):
            last = jnp.concatenate(part(powers[-1], i, k), axis=0)
            highs, lows = stacked(powers, i, k)
            with_high += lax.dot_general(last, highs, NT, preferred_element_type=f32)
            with_low += lax.dot_general(last, lows, NT, preferred_element_type=f32)
    return with_high[:BLOCK] + (with_high[BLOCK:] + with_low[:BLOCK] + with_low[BLOCK:])


def powers_of(refs):
    return [refs[at : at + 2] for at in range(0, len(refs), 2)]


def local_kernel(high, low, *refs):
    powers, (partial, row) = powers_of(refs[:-2]), refs[-2:]
    for i in range(2):
        for k in range(2):
            sources = [part(powers[-1], *at) for at in ((i, k), (1 - i, k), (i, 1 - k))]
            partial[i, k] = times(high[2 * i + k], low[2 * i + k], sources)
    row[...] = gram_row(powers)


def select(flag, yes, no):
    return jnp.where(flag > 0, yes, no)


def early_kernel(partial, even, sibling, both_high, both_low, high, low, middle):
    middle[0] = partial[0, 1] + times(high[0], low[0], [split(even[0])])
    middle[1] = partial[1, 0] + times(high[1], low[1], [split(sibling[0])])
    sources = [split(sibling[1]), split(even[1])]
    middle[2] = partial[1, 1] + times(both_high[1], both_low[1], sources)


def next_power(scale, flags, odd, across, partial, middle, both_high, both_low, high, low):
    odds = [split(select(flags[1:2], odd[i], 0.0)) for i in range(2)]
    acrosses = [split(select(flags[0:1], across[k], 0.0)) for k in range(2)]
    corner = partial[0, 0] + times(both_high[0], both_low[0], [acrosses[0], odds[0]])
    beside = middle[0] + times(high[0], low[0], [acrosses[1]])
    below = middle[1] + times(high[1], low[1], [odds[1]])
    factor = scale / basis_scale
    return [[corner * factor, beside * factor], [below * factor, middle[2] * factor]]


def emit(values, high, low, to_odd, to_even, to_across, to_sibling):
    for i in range(2):
        to_odd[i], to_even[i] = values[i][0], values[i][1]
        to_across[i], to_sibling[i] = values[0][i], values[1][i]
    for i in range(2):
        for k in range(2):
            high[i, k], low[i, k] = split(values[i][k])


def late_kernel(scale, *refs):
    emit(next_power(scale, *refs[:9]), *refs[9:])


def last_kernel(scale, *refs):
    inputs, refs, outs = refs[:9], refs[9:-4], refs[-4:]
    rows, powers = refs[: SPAN - 1], powers_of(refs[SPAN - 1 :])
    last_high, last_low, keep, send = outs
    values = next_power(scale, *inputs)
    last = {}
    for i in range(2):
        for k in range(2):
            last[i, k] = split(values[i][k])
            last_high[i, k], last_low[i, k] = last[i, k]
    powers.append([{at: parts[j] for at, parts in last.items()} for j in range(2)])
    pack(inputs[0], [row[...] for row in rows] + [gram_row(powers)], keep, send)


def start_kernel(flags, forcing, *outs):
    field = [[forcing[:, w, s, :] for s in range(2)] for w in range(2)]
    emit(turned(flags[4:5], flags[5:6], field), *outs)


def turned(core, parity, field):
    field = [[select(core, field[1 - i][k], field[i][k]) for k in range(2)] for i in range(2)]
    return [[select(parity, line[1 - k], line[k]) for k in range(2)] for line in field]


PAIR = [shape(2, 2, BLOCK, ROWS, dtype=bf16)] * 2
FIELD = PAIR + [shape(2, BLOCK, ROWS)] * 4


def pack(flags, lines, keep, send):
    last = lines[8]
    first_half = jnp.concatenate(
        [last[:, :128], lines[7], jnp.concatenate([lines[6], lines[0]], axis=1)], axis=0
    )
    second_half = jnp.concatenate(
        [
            jnp.concatenate([lines[5], lines[1]], axis=1),
            jnp.concatenate([lines[4], lines[2]], axis=1),
            jnp.concatenate([lines[3], last[:, 128:], jnp.zeros((BLOCK, 48), f32)], axis=1),
        ],
        axis=0,
    )
    core = flags[4:5, :128]
    keep[...] = select(core, second_half, first_half)
    send[...] = select(core, first_half, second_half)


def unpack_gram(first, second):
    lines = [
        first[32:48, 112:],
        second[:16, 96:],
        second[16:32, 80:],
        second[32:48, :64],
        second[16:32, :80],
        second[:16, :96],
        first[32:48, :112],
        first[16:32],
        jnp.concatenate([first[:16], second[32:48, 64:80]], axis=1),
    ]
    lower = jnp.concatenate(
        [
            line
            if line.shape[1] == WIDTH
            else jnp.concatenate([line, jnp.zeros((BLOCK, WIDTH - line.shape[1]), f32)], axis=1)
            for line in lines
        ],
        axis=0,
    )
    row = lax.broadcasted_iota(jnp.int32, (WIDTH, WIDTH), 0) // BLOCK
    column = lax.broadcasted_iota(jnp.int32, (WIDTH, WIDTH), 1) // BLOCK
    return jnp.where(row >= column, lower, lower.T)


def small_solve(gram):
    right = basis_shift * gram[:, :INNER] + basis_scale * gram[:, BLOCK:]
    normal = basis_shift * right[:INNER] + basis_scale * right[BLOCK:]
    target = basis_shift * gram[:INNER, :BLOCK] + basis_scale * gram[BLOCK:, :BLOCK]
    system = jnp.concatenate([normal, target, jnp.zeros((INNER, 48), f32)], axis=1)
    rows = lax.broadcasted_iota(jnp.int32, (INNER, 128), 0)
    group = 8
    for start in range(0, INNER, group):
        columns = [
            jnp.broadcast_to(system[:, start + j : start + j + 1], (INNER, 128))
            for j in range(group)
        ]
        for j in range(group):
            k = start + j
            inverse = 1.0 / columns[j][k : k + 1]
            pivot_row = system[k : k + 1] * inverse
            system = jnp.where(rows == k, pivot_row, system - columns[j] * pivot_row)
            for later in range(j + 1, group):
                scaled = columns[later][k : k + 1] * inverse
                columns[later] = jnp.where(
                    rows == k, scaled, columns[later] - columns[j] * scaled
                )
    coefficients = system[:, INNER:PANEL]
    zero = jnp.zeros((BLOCK, BLOCK), f32)
    update = basis_shift * jnp.concatenate([coefficients, zero], axis=0)
    update = update + basis_scale * jnp.concatenate([zero, coefficients], axis=0)
    return coefficients, update


def add_spread_kernel(own, other, copies):
    copies[...] = jnp.broadcast_to((own[...] + other[...])[None], copies.shape)


def sum_spread_kernel(received, copies):
    copies[...] = jnp.broadcast_to(jnp.sum(received[...], axis=0)[None], copies.shape)


def sum_kernel(received, total):
    total[...] = jnp.sum(received[...], axis=0)


def device_sum(keep, send):
    half = PACKED // 2
    other = lax.ppermute(send, AXES, SIBLING)
    copies = call(add_spread_kernel, "join", shape(16, half, 128), (keep, other), 10**6)
    received = lax.all_to_all(copies, AXES, 0, 0, axis_index_groups=PLANE)
    copies = call(sum_spread_kernel, "resum", shape(8, half, 128), (received,), 10**6)
    received = lax.all_to_all(copies, AXES, 0, 0, axis_index_groups=DEPTH)
    total = call(sum_kernel, "sum", shape(half, 128), (received,), 10**6)
    return total, lax.ppermute(total, AXES, SIBLING)


def dot(left, right, dims=(((1,), (0,)), ((), ()))):
    return lax.dot_general(left, right, dims, precision=highest, preferred_element_type=f32)


def finish_kernel(flags, own, other, *refs):
    powers, (solution_out, residual_out) = powers_of(refs[:-2]), refs[-2:]
    core = flags[4:5, :128]
    own, other = own[...], other[...]
    gram = unpack_gram(select(core, other, own), select(core, own, other))
    coefficients, update = small_solve(gram[:PANEL, :PANEL])
    row = lax.broadcasted_iota(jnp.int32, (BLOCK, PANEL), 0)
    column = lax.broadcasted_iota(jnp.int32, (BLOCK, PANEL), 1)
    identity = jnp.where(row == column, 1.0, 0.0)
    remainder = identity - update.T
    zeros = lambda width: [jnp.zeros((BLOCK, width), f32)] if width else []
    mixing = jnp.concatenate(
        [
            jnp.concatenate(
                zeros(BLOCK * j) + [remainder] + zeros(WIDTH - PANEL - BLOCK * j), axis=1
            )
            for j in range(STEPS + 1)
        ],
        axis=0,
    )
    power = lax.broadcasted_iota(jnp.int32, (PANEL, WIDTH), 1) // BLOCK
    for j in range(STEPS + 1, SPAN):
        mixing = jnp.where(power == j, mixing * GROWTH ** (STEPS - j), mixing)
    second_gram = dot(dot(mixing, gram), mixing, NT)
    second_coefficients, second_update = small_solve(second_gram)
    first_weights = jnp.concatenate([coefficients.T] + zeros(WIDTH - INNER), axis=1)
    second = jnp.concatenate(
        [
            jnp.concatenate([second_coefficients.T] + zeros(BLOCK), axis=1),
            identity - second_update.T,
        ],
        axis=0,
    )
    weights = dot(second, mixing)
    weights = jnp.concatenate([weights[:BLOCK] + first_weights, weights[BLOCK:]], axis=0)
    first, rest = split(weights)
    third = (weights - first.astype(f32) - rest.astype(f32)).astype(bf16)
    parts = jnp.concatenate([first, rest, third], axis=0)
    count = 2 * BLOCK
    plain = (((1,), (0,)), ((), ()))
    mixed = [[None, None], [None, None]]
    for i in range(2):
        for k in range(2):
            highs, lows = stacked(powers, i, k)
            of_high = lax.dot_general(parts, highs, plain, preferred_element_type=f32)
            of_low = lax.dot_general(parts[: 2 * count], lows, plain, preferred_element_type=f32)
            small = of_high[count : 2 * count] + of_low[:count]
            small = small + (of_high[2 * count :] + of_low[count:])
            mixed[i][k] = of_high[:count] + small
    mixed = turned(flags[4:5], flags[5:6], mixed)
    for w in range(2):
        for s in range(2):
            solution_out[:, w, s, :] = mixed[w][s][:BLOCK]
            residual_out[:, w, s, :] = mixed[w][s][BLOCK:]


def on_device(forcing, diag_blocks, coupling):
    wall, stream = lax.axis_index("wall"), lax.axis_index("stream")
    core, parity = wall % 2 > 0, stream % 2 > 0
    across_inside = jnp.where(core, wall < 7, wall > 0)
    odd_inside = jnp.where(parity, stream < 31, stream > 0)
    flags = jnp.stack([across_inside, odd_inside, False, False, core, parity, False, False])
    flags = jnp.broadcast_to(flags.astype(f32)[:, None], (8, ROWS))
    field = call(start_kernel, "start", FIELD, (flags, forcing), 10**6)
    own_parts, both_parts, early_parts, late_parts = prepare(diag_blocks, coupling)
    powers, rows = [*field[:2]], []
    for step in range(2 * STEPS):
        to_odd, to_even, to_across, to_sibling = field[2:]
        odd = lax.ppermute(to_odd, AXES, ODD)
        even = lax.ppermute(to_even, AXES, EVEN)
        across = lax.ppermute(to_across, AXES, ACROSS)
        sibling = lax.ppermute(to_sibling, AXES, SIBLING)
        partial, row = call(
            local_kernel,
            "local",
            [shape(2, 2, BLOCK, ROWS), shape(BLOCK, BLOCK * (step + 1))],
            (*own_parts, *powers),
            10**9,
        )
        rows.append(row)
        middle = call(
            early_kernel,
            "early",
            shape(3, BLOCK, ROWS),
            (partial, even, sibling, *both_parts, *early_parts),
            10**9,
        )
        scale = 1.0 if step < STEPS else GROWTH
        operands = (flags, odd, across, partial, middle, *both_parts, *late_parts)
        if step < 2 * STEPS - 1:
            kernel = functools.partial(late_kernel, scale)
            field = call(kernel, "late", FIELD, operands, 10**9)
            powers += field[:2]
    *last, keep, send = call(
        functools.partial(last_kernel, scale),
        "last",
        PAIR + [shape(PACKED // 2, 128)] * 2,
        (*operands, *rows, *powers),
        10**9,
    )
    powers += last
    own, other = device_sum(keep, send)
    return call(
        finish_kernel,
        "finish",
        [jax.ShapeDtypeStruct((BLOCK, 2, 2, ROWS), f32)] * 2,
        (flags, own, other, *powers),
        10**8,
    )


def solution(mesh):
    return jax.shard_map(
        on_device,
        mesh=mesh,
        in_specs=(
            P(None, "wall", "stream", None),
            P("wall", "stream", None, None),
            P(None, "wall", "stream", None, None),
        ),
        out_specs=(P(None, "wall", "stream", None), P(None, "wall", "stream", None)),
        check_vma=False,
    )
```

```python
import functools

import jax
import jax.numpy as jnp
from jax import lax
from jax.experimental import pallas as pl
from jax.experimental.pallas import tpu as pltpu
from jax.sharding import PartitionSpec as P

ROWS = 320
BLOCK = 16
STEPS = 4
PANEL = 80
INNER = PANEL - BLOCK
SPAN = 2 * STEPS + 1
basis_shift = 1.5
basis_scale = 0.8

f32 = jnp.float32
bf16 = jnp.bfloat16
highest = lax.Precision.HIGHEST
AXES = ("wall", "stream")
NT = (((1,), (1,)), ((), ()))
VMEM = pl.BlockSpec(memory_space=pltpu.VMEM)


def groups_by(key):
    found = {}
    for wall in range(8):
        for stream in range(32):
            place = key(wall // 2, wall % 2, stream % 4, stream // 4)
            found.setdefault(place, []).append(wall * 32 + stream)
    return list(found.values())


PLANE = groups_by(lambda x, core, y, z: (core, z))
DEPTH = groups_by(lambda x, core, y, z: (core, x, y))


def partners(partner):
    pairs = []
    for wall in range(8):
        for stream in range(32):
            other_wall, other_stream = partner(wall, stream)
            pairs.append((wall * 32 + stream, other_wall % 8 * 32 + other_stream % 32))
    return pairs


SIBLING = partners(lambda w, s: (w ^ 1, s))
ACROSS = partners(lambda w, s: (w - 1 + 2 * (w % 2), s))
EVEN = partners(lambda w, s: (w, s ^ 1))
ODD = partners(lambda w, s: (w, s - 1 + 2 * (s % 2)))
WIDTH = SPAN * BLOCK
PACKED = 96
GROWTH = 2.0**-4


def call(kernel, name, out_shape, operands, flops):
    return pl.pallas_call(
        kernel,
        in_specs=[VMEM] * len(operands),
        out_specs=jax.tree.map(lambda _: VMEM, out_shape),
        out_shape=out_shape,
        compiler_params=pltpu.CompilerParams(vmem_limit_bytes=8 * 2**20),
        cost_estimate=pl.CostEstimate(flops=flops, bytes_accessed=2**20, transcendentals=0),
        name=name,
    )(*operands)


def shape(*dims, dtype=f32):
    return pltpu.VMEM(dims, dtype)


def split(value):
    high = value.astype(bf16)
    return high, (value - high.astype(f32)).astype(bf16)


def place(i, k):
    core, parity = lax.axis_index("wall") % 2, lax.axis_index("stream") % 2
    return (1 - core if i else core), (1 - parity if k else parity)


def prepare_kernel(diag, coupling, *refs):
    outs, (raw, arrived) = refs[:8], refs[8:]
    row = lax.broadcasted_iota(jnp.int32, (ROWS, ROWS), 0)
    column = lax.broadcasted_iota(jnp.int32, (ROWS, ROWS), 1)
    shift = jnp.where(row == column, basis_shift, 0.0)
    fetches, targets = [], []
    for i in range(2):
        for k in range(2):
            wall, stream = place(i, k)
            blocks = [diag.at[wall, stream]]
            for face in (1 - wall, 3 - stream, wall, 2 + stream):
                blocks.append(coupling.at[face, wall, stream])
            for block in blocks:
                slot = len(fetches)
                fetches.append(pltpu.make_async_copy(block, raw.at[slot], arrived.at[slot]))
            targets += [(0, 2 * i + k, at) for at in range(3)]
            if i == k:
                targets += [(2, i, 0), (2, i, 1)]
            else:
                targets += [(6, 0, 0), (4, 0, 0)] if k else [(4, 1, 0), (6, 1, 0)]
    for fetch in fetches:
        fetch.start()
    for slot, (out, index, at) in enumerate(targets):
        fetches[slot].wait()
        block = raw[slot]
        high_part, low_part = split(block - shift if slot % 5 == 0 else block)
        outs[out][index, :, at * ROWS : (at + 1) * ROWS] = high_part
        outs[out + 1][index, :, at * ROWS : (at + 1) * ROWS] = low_part


def prepare(diag_blocks, coupling):
    sizes = [(4, 3), (2, 2), (2, 1), (2, 1)]
    parts = pl.pallas_call(
        prepare_kernel,
        in_specs=[pl.BlockSpec(memory_space=pltpu.HBM)] * 2,
        out_specs=[VMEM] * 8,
        out_shape=[shape(n, ROWS, m * ROWS, dtype=bf16) for n, m in sizes for _ in range(2)],
        scratch_shapes=[pltpu.VMEM((20, ROWS, ROWS), f32), pltpu.SemaphoreType.DMA((20,))],
        compiler_params=pltpu.CompilerParams(vmem_limit_bytes=24 * 2**20),
        cost_estimate=pl.CostEstimate(flops=0, bytes_accessed=2**24, transcendentals=0),
        name="prepare",
    )(
        pltpu.with_memory_space_constraint(diag_blocks, pltpu.HBM),
        pltpu.with_memory_space_constraint(coupling, pltpu.HBM),
    )
    return parts[0:2], parts[2:4], parts[4:6], parts[6:8]


def times(high, low, sources):
    highs, lows = zip(*sources)
    high_source = jnp.concatenate(highs, axis=1)
    both = jnp.concatenate([high_source, jnp.concatenate(lows, axis=1)], axis=0)
    first = lax.dot_general(both, high, NT, preferred_element_type=f32)
    second = lax.dot_general(high_source, low, NT, preferred_element_type=f32)
    return first[:BLOCK] + (first[BLOCK:] + second)


def part(power, i, k):
    return power[0][i, k], power[1][i, k]


def stacked(powers, i, k):
    highs, lows = zip(*[part(power, i, k) for power in powers])
    return jnp.concatenate(highs, axis=0), jnp.concatenate(lows, axis=0)


def gram_row(powers):
    with_high, with_low = 0.0, 0.0
    for i in range(2):
        for k in range(2):
            last = jnp.concatenate(part(powers[-1], i, k), axis=0)
            highs, lows = stacked(powers, i, k)
            with_high += lax.dot_general(last, highs, NT, preferred_element_type=f32)
            with_low += lax.dot_general(last, lows, NT, preferred_element_type=f32)
    return with_high[:BLOCK] + (with_high[BLOCK:] + with_low[:BLOCK] + with_low[BLOCK:])


def powers_of(refs):
    return [refs[at : at + 2] for at in range(0, len(refs), 2)]


def local_kernel(high, low, *refs):
    powers, (partial, row) = powers_of(refs[:-2]), refs[-2:]
    for i in range(2):
        for k in range(2):
            sources = [part(powers[-1], *at) for at in ((i, k), (1 - i, k), (i, 1 - k))]
            partial[i, k] = times(high[2 * i + k], low[2 * i + k], sources)
    row[...] = gram_row(powers)


def select(flag, yes, no):
    return jnp.where(flag > 0, yes, no)


def early_kernel(partial, even, sibling, both_high, both_low, high, low, middle):
    middle[0] = partial[0, 1] + times(high[0], low[0], [split(even[0])])
    middle[1] = partial[1, 0] + times(high[1], low[1], [split(sibling[0])])
    sources = [split(sibling[1]), split(even[1])]
    middle[2] = partial[1, 1] + times(both_high[1], both_low[1], sources)


def next_power(scale, flags, odd, middle, across, partial, both_high, both_low, high, low):
    odds = [split(select(flags[1:2], odd[i], 0.0)) for i in range(2)]
    acrosses = [split(select(flags[0:1], across[k], 0.0)) for k in range(2)]
    corner = partial[0, 0] + times(both_high[0], both_low[0], [acrosses[0], odds[0]])
    beside = middle[0] + times(high[0], low[0], [acrosses[1]])
    below = middle[1] + times(high[1], low[1], [odds[1]])
    factor = scale / basis_scale
    return [[corner * factor, beside * factor], [below * factor, middle[2] * factor]]


def emit(values, high, low, to_odd, to_even, to_across, to_sibling):
    for i in range(2):
        to_odd[i], to_even[i] = values[i][0], values[i][1]
        to_across[i], to_sibling[i] = values[0][i], values[1][i]
    for i in range(2):
        for k in range(2):
            high[i, k], low[i, k] = split(values[i][k])


def late_kernel(scale, *refs):
    emit(next_power(scale, *refs[:9]), *refs[9:])


def last_kernel(scale, *refs):
    inputs, refs, outs = refs[:9], refs[9:-4], refs[-4:]
    rows, powers = refs[: SPAN - 1], powers_of(refs[SPAN - 1 :])
    last_high, last_low, keep, send = outs
    values = next_power(scale, *inputs)
    last = {}
    for i in range(2):
        for k in range(2):
            last[i, k] = split(values[i][k])
            last_high[i, k], last_low[i, k] = last[i, k]
    powers.append([{at: parts[j] for at, parts in last.items()} for j in range(2)])
    pack(inputs[0], [row[...] for row in rows] + [gram_row(powers)], keep, send)


def start_kernel(flags, forcing, *outs):
    field = [[forcing[:, w, s, :] for s in range(2)] for w in range(2)]
    emit(turned(flags[4:5], flags[5:6], field), *outs)


def turned(core, parity, field):
    field = [[select(core, field[1 - i][k], field[i][k]) for k in range(2)] for i in range(2)]
    return [[select(parity, line[1 - k], line[k]) for k in range(2)] for line in field]


PAIR = [shape(2, 2, BLOCK, ROWS, dtype=bf16)] * 2
FIELD = PAIR + [shape(2, BLOCK, ROWS)] * 4


def pack(flags, lines, keep, send):
    last = lines[8]
    first_half = jnp.concatenate(
        [last[:, :128], lines[7], jnp.concatenate([lines[6], lines[0]], axis=1)], axis=0
    )
    second_half = jnp.concatenate(
        [
            jnp.concatenate([lines[5], lines[1]], axis=1),
            jnp.concatenate([lines[4], lines[2]], axis=1),
            jnp.concatenate([lines[3], last[:, 128:], jnp.zeros((BLOCK, 48), f32)], axis=1),
        ],
        axis=0,
    )
    core = flags[4:5, :128]
    keep[...] = select(core, second_half, first_half)
    send[...] = select(core, first_half, second_half)


def unpack_gram(first, second):
    lines = [
        first[32:48, 112:],
        second[:16, 96:],
        second[16:32, 80:],
        second[32:48, :64],
        second[16:32, :80],
        second[:16, :96],
        first[32:48, :112],
        first[16:32],
        jnp.concatenate([first[:16], second[32:48, 64:80]], axis=1),
    ]
    lower = jnp.concatenate(
        [
            line
            if line.shape[1] == WIDTH
            else jnp.concatenate([line, jnp.zeros((BLOCK, WIDTH - line.shape[1]), f32)], axis=1)
            for line in lines
        ],
        axis=0,
    )
    row = lax.broadcasted_iota(jnp.int32, (WIDTH, WIDTH), 0) // BLOCK
    column = lax.broadcasted_iota(jnp.int32, (WIDTH, WIDTH), 1) // BLOCK
    return jnp.where(row >= column, lower, lower.T)


def small_solve(gram):
    right = basis_shift * gram[:, :INNER] + basis_scale * gram[:, BLOCK:]
    normal = basis_shift * right[:INNER] + basis_scale * right[BLOCK:]
    target = basis_shift * gram[:INNER, :BLOCK] + basis_scale * gram[BLOCK:, :BLOCK]
    system = jnp.concatenate([normal, target, jnp.zeros((INNER, 48), f32)], axis=1)
    rows = lax.broadcasted_iota(jnp.int32, (INNER, 128), 0)
    group = 8
    for start in range(0, INNER, group):
        columns = [
            jnp.broadcast_to(system[:, start + j : start + j + 1], (INNER, 128))
            for j in range(group)
        ]
        for j in range(group):
            k = start + j
            inverse = 1.0 / columns[j][k : k + 1]
            pivot_row = system[k : k + 1] * inverse
            system = jnp.where(rows == k, pivot_row, system - columns[j] * pivot_row)
            for later in range(j + 1, group):
                scaled = columns[later][k : k + 1] * inverse
                columns[later] = jnp.where(
                    rows == k, scaled, columns[later] - columns[j] * scaled
                )
    coefficients = system[:, INNER:PANEL]
    zero = jnp.zeros((BLOCK, BLOCK), f32)
    update = basis_shift * jnp.concatenate([coefficients, zero], axis=0)
    update = update + basis_scale * jnp.concatenate([zero, coefficients], axis=0)
    return coefficients, update


def add_spread_kernel(own, other, copies):
    copies[...] = jnp.broadcast_to((own[...] + other[...])[None], copies.shape)


def sum_spread_kernel(received, copies):
    copies[...] = jnp.broadcast_to(jnp.sum(received[...], axis=0)[None], copies.shape)


def sum_kernel(received, total):
    total[...] = jnp.sum(received[...], axis=0)


def device_sum(keep, send):
    half = PACKED // 2
    other = lax.ppermute(send, AXES, SIBLING)
    copies = call(add_spread_kernel, "join", shape(16, half, 128), (keep, other), 10**6)
    received = lax.all_to_all(copies, AXES, 0, 0, axis_index_groups=PLANE)
    copies = call(sum_spread_kernel, "resum", shape(8, half, 128), (received,), 10**6)
    received = lax.all_to_all(copies, AXES, 0, 0, axis_index_groups=DEPTH)
    total = call(sum_kernel, "sum", shape(half, 128), (received,), 10**6)
    return total, lax.ppermute(total, AXES, SIBLING)


def dot(left, right, dims=(((1,), (0,)), ((), ()))):
    return lax.dot_general(left, right, dims, precision=highest, preferred_element_type=f32)


def finish_kernel(flags, own, other, *refs):
    powers, (solution_out, residual_out) = powers_of(refs[:-2]), refs[-2:]
    core = flags[4:5, :128]
    own, other = own[...], other[...]
    gram = unpack_gram(select(core, other, own), select(core, own, other))
    coefficients, update = small_solve(gram[:PANEL, :PANEL])
    row = lax.broadcasted_iota(jnp.int32, (BLOCK, PANEL), 0)
    column = lax.broadcasted_iota(jnp.int32, (BLOCK, PANEL), 1)
    identity = jnp.where(row == column, 1.0, 0.0)
    remainder = identity - update.T
    zeros = lambda width: [jnp.zeros((BLOCK, width), f32)] if width else []
    mixing = jnp.concatenate(
        [
            jnp.concatenate(
                zeros(BLOCK * j) + [remainder] + zeros(WIDTH - PANEL - BLOCK * j), axis=1
            )
            for j in range(STEPS + 1)
        ],
        axis=0,
    )
    power = lax.broadcasted_iota(jnp.int32, (PANEL, WIDTH), 1) // BLOCK
    for j in range(STEPS + 1, SPAN):
        mixing = jnp.where(power == j, mixing * GROWTH ** (STEPS - j), mixing)
    second_gram = dot(dot(mixing, gram), mixing, NT)
    second_coefficients, second_update = small_solve(second_gram)
    first_weights = jnp.concatenate([coefficients.T] + zeros(WIDTH - INNER), axis=1)
    second = jnp.concatenate(
        [
            jnp.concatenate([second_coefficients.T] + zeros(BLOCK), axis=1),
            identity - second_update.T,
        ],
        axis=0,
    )
    weights = dot(second, mixing)
    weights = jnp.concatenate([weights[:BLOCK] + first_weights, weights[BLOCK:]], axis=0)
    first, rest = split(weights)
    third = (weights - first.astype(f32) - rest.astype(f32)).astype(bf16)
    parts = jnp.concatenate([first, rest, third], axis=0)
    count = 2 * BLOCK
    plain = (((1,), (0,)), ((), ()))
    mixed = [[None, None], [None, None]]
    for i in range(2):
        for k in range(2):
            highs, lows = stacked(powers, i, k)
            of_high = lax.dot_general(parts, highs, plain, preferred_element_type=f32)
            of_low = lax.dot_general(parts[: 2 * count], lows, plain, preferred_element_type=f32)
            small = of_high[count : 2 * count] + of_low[:count]
            small = small + (of_high[2 * count :] + of_low[count:])
            mixed[i][k] = of_high[:count] + small
    mixed = turned(flags[4:5], flags[5:6], mixed)
    for w in range(2):
        for s in range(2):
            solution_out[:, w, s, :] = mixed[w][s][:BLOCK]
            residual_out[:, w, s, :] = mixed[w][s][BLOCK:]


def on_device(forcing, diag_blocks, coupling):
    wall, stream = lax.axis_index("wall"), lax.axis_index("stream")
    core, parity = wall % 2 > 0, stream % 2 > 0
    across_inside = jnp.where(core, wall < 7, wall > 0)
    odd_inside = jnp.where(parity, stream < 31, stream > 0)
    flags = jnp.stack([across_inside, odd_inside, False, False, core, parity, False, False])
    flags = jnp.broadcast_to(flags.astype(f32)[:, None], (8, ROWS))
    field = call(start_kernel, "start", FIELD, (flags, forcing), 10**6)
    own_parts, both_parts, early_parts, late_parts = prepare(diag_blocks, coupling)
    powers, rows = [*field[:2]], []
    for step in range(2 * STEPS):
        to_odd, to_even, to_across, to_sibling = field[2:]
        odd = lax.ppermute(to_odd, AXES, ODD)
        even = lax.ppermute(to_even, AXES, EVEN)
        across = lax.ppermute(to_across, AXES, ACROSS)
        sibling = lax.ppermute(to_sibling, AXES, SIBLING)
        partial, row = call(
            local_kernel,
            "local",
            [shape(2, 2, BLOCK, ROWS), shape(BLOCK, BLOCK * (step + 1))],
            (*own_parts, *powers),
            10**9,
        )
        rows.append(row)
        middle = call(
            early_kernel,
            "early",
            shape(3, BLOCK, ROWS),
            (partial, even, sibling, *both_parts, *early_parts),
            10**9,
        )
        scale = 1.0 if step < STEPS else GROWTH
        operands = (flags, odd, middle, across, partial, *both_parts, *late_parts)
        if step < 2 * STEPS - 1:
            kernel = functools.partial(late_kernel, scale)
            field = call(kernel, "late", FIELD, operands, 10**9)
            powers += field[:2]
    *last, keep, send = call(
        functools.partial(last_kernel, scale),
        "last",
        PAIR + [shape(PACKED // 2, 128)] * 2,
        (*operands, *rows, *powers),
        10**9,
    )
    powers += last
    own, other = device_sum(keep, send)
    return call(
        finish_kernel,
        "finish",
        [jax.ShapeDtypeStruct((BLOCK, 2, 2, ROWS), f32)] * 2,
        (flags, own, other, *powers),
        10**8,
    )


def solution(mesh):
    return jax.shard_map(
        on_device,
        mesh=mesh,
        in_specs=(
            P(None, "wall", "stream", None),
            P("wall", "stream", None, None),
            P(None, "wall", "stream", None, None),
        ),
        out_specs=(P(None, "wall", "stream", None), P(None, "wall", "stream", None)),
        check_vma=False,
    )
```

```python
import functools

import jax
import jax.numpy as jnp
from jax import lax
from jax.experimental import pallas as pl
from jax.experimental.pallas import tpu as pltpu
from jax.sharding import PartitionSpec as P

ROWS = 320
BLOCK = 16
STEPS = 4
PANEL = 80
INNER = PANEL - BLOCK
SPAN = 2 * STEPS + 1
basis_shift = 1.5
basis_scale = 0.8

f32 = jnp.float32
bf16 = jnp.bfloat16
highest = lax.Precision.HIGHEST
AXES = ("wall", "stream")
NT = (((1,), (1,)), ((), ()))
VMEM = pl.BlockSpec(memory_space=pltpu.VMEM)


def groups_by(key):
    found = {}
    for wall in range(8):
        for stream in range(32):
            place = key(wall // 2, wall % 2, stream % 4, stream // 4)
            found.setdefault(place, []).append(wall * 32 + stream)
    return list(found.values())


PLANE = groups_by(lambda x, core, y, z: (core, z))
DEPTH = groups_by(lambda x, core, y, z: (core, x, y))


def partners(partner):
    pairs = []
    for wall in range(8):
        for stream in range(32):
            other_wall, other_stream = partner(wall, stream)
            pairs.append((wall * 32 + stream, other_wall % 8 * 32 + other_stream % 32))
    return pairs


SIBLING = partners(lambda w, s: (w ^ 1, s))
ACROSS = partners(lambda w, s: (w - 1 + 2 * (w % 2), s))
EVEN = partners(lambda w, s: (w, s ^ 1))
ODD = partners(lambda w, s: (w, s - 1 + 2 * (s % 2)))
WIDTH = SPAN * BLOCK
PACKED = 96
GROWTH = 2.0**-4


def call(kernel, name, out_shape, operands, flops):
    return pl.pallas_call(
        kernel,
        in_specs=[VMEM] * len(operands),
        out_specs=jax.tree.map(lambda _: VMEM, out_shape),
        out_shape=out_shape,
        compiler_params=pltpu.CompilerParams(vmem_limit_bytes=8 * 2**20),
        cost_estimate=pl.CostEstimate(flops=flops, bytes_accessed=2**20, transcendentals=0),
        name=name,
    )(*operands)


def shape(*dims, dtype=f32):
    return pltpu.VMEM(dims, dtype)


def split(value):
    high = value.astype(bf16)
    return high, (value - high.astype(f32)).astype(bf16)


def place(i, k):
    core, parity = lax.axis_index("wall") % 2, lax.axis_index("stream") % 2
    return (1 - core if i else core), (1 - parity if k else parity)


def prepare_kernel(diag, coupling, *refs):
    outs, (raw, arrived) = refs[:10], refs[10:]
    row = lax.broadcasted_iota(jnp.int32, (ROWS, ROWS), 0)
    column = lax.broadcasted_iota(jnp.int32, (ROWS, ROWS), 1)
    shift = jnp.where(row == column, basis_shift, 0.0)
    fetches, targets = [], []
    for i in range(2):
        for k in range(2):
            wall, stream = place(i, k)
            blocks = [diag.at[wall, stream]]
            for face in (1 - wall, 3 - stream, wall, 2 + stream):
                blocks.append(coupling.at[face, wall, stream])
            for block in blocks:
                slot = len(fetches)
                fetches.append(pltpu.make_async_copy(block, raw.at[slot], arrived.at[slot]))
            targets += [(0, 2 * i + k, at) for at in range(3)]
            if i == k == 0:
                targets += [(2, 0, 0), (2, 0, 1)]
            else:
                targets += [(6, k, 0) if i else (8, 0, 0), (4, i, 0) if k else (8, 1, 0)]
    for fetch in fetches:
        fetch.start()
    for slot, (out, index, at) in enumerate(targets):
        fetches[slot].wait()
        block = raw[slot]
        high_part, low_part = split(block - shift if slot % 5 == 0 else block)
        outs[out][index, :, at * ROWS : (at + 1) * ROWS] = high_part
        outs[out + 1][index, :, at * ROWS : (at + 1) * ROWS] = low_part


def prepare(diag_blocks, coupling):
    sizes = [(4, 3), (1, 2), (2, 1), (2, 1), (2, 1)]
    parts = pl.pallas_call(
        prepare_kernel,
        in_specs=[pl.BlockSpec(memory_space=pltpu.HBM)] * 2,
        out_specs=[VMEM] * 10,
        out_shape=[shape(n, ROWS, m * ROWS, dtype=bf16) for n, m in sizes for _ in range(2)],
        scratch_shapes=[pltpu.VMEM((20, ROWS, ROWS), f32), pltpu.SemaphoreType.DMA((20,))],
        compiler_params=pltpu.CompilerParams(vmem_limit_bytes=24 * 2**20),
        cost_estimate=pl.CostEstimate(flops=0, bytes_accessed=2**24, transcendentals=0),
        name="prepare",
    )(
        pltpu.with_memory_space_constraint(diag_blocks, pltpu.HBM),
        pltpu.with_memory_space_constraint(coupling, pltpu.HBM),
    )
    return [parts[at : at + 2] for at in range(0, 10, 2)]


def times(high, low, sources):
    highs, lows = zip(*sources)
    high_source = jnp.concatenate(highs, axis=1)
    both = jnp.concatenate([high_source, jnp.concatenate(lows, axis=1)], axis=0)
    first = lax.dot_general(both, high, NT, preferred_element_type=f32)
    second = lax.dot_general(high_source, low, NT, preferred_element_type=f32)
    return first[:BLOCK] + (first[BLOCK:] + second)


def part(power, i, k):
    return power[0][i, k], power[1][i, k]


def stacked(powers, i, k):
    highs, lows = zip(*[part(power, i, k) for power in powers])
    return jnp.concatenate(highs, axis=0), jnp.concatenate(lows, axis=0)


def gram_row(powers):
    with_high, with_low = 0.0, 0.0
    for i in range(2):
        for k in range(2):
            last = jnp.concatenate(part(powers[-1], i, k), axis=0)
            highs, lows = stacked(powers, i, k)
            with_high += lax.dot_general(last, highs, NT, preferred_element_type=f32)
            with_low += lax.dot_general(last, lows, NT, preferred_element_type=f32)
    return with_high[:BLOCK] + (with_high[BLOCK:] + with_low[:BLOCK] + with_low[BLOCK:])


def powers_of(refs):
    return [refs[at : at + 2] for at in range(0, len(refs), 2)]


def local_kernel(high, low, *refs):
    powers, (partial, row) = powers_of(refs[:-2]), refs[-2:]
    for i in range(2):
        for k in range(2):
            sources = [part(powers[-1], *at) for at in ((i, k), (1 - i, k), (i, 1 - k))]
            partial[i, k] = times(high[2 * i + k], low[2 * i + k], sources)
    row[...] = gram_row(powers)


def select(flag, yes, no):
    return jnp.where(flag > 0, yes, no)


def even_kernel(partial, even, high, low, middle):
    for i in range(2):
        middle[i] = partial[i, 1] + times(high[i], low[i], [split(even[i])])


def sibling_kernel(partial, middle, sibling, high, low, below):
    for k, before in enumerate((partial[1, 0], middle[1])):
        below[k] = before + times(high[k], low[k], [split(sibling[k])])


def next_power(scale, flags, odd, middle, across, below, partial, corner, high, low):
    odds = [split(select(flags[1:2], odd[i], 0.0)) for i in range(2)]
    acrosses = [split(select(flags[0:1], across[k], 0.0)) for k in range(2)]
    first = partial[0, 0] + times(corner[0][0], corner[1][0], [acrosses[0], odds[0]])
    beside = middle[0] + times(high[0], low[0], [acrosses[1]])
    under = below[0] + times(high[1], low[1], [odds[1]])
    factor = scale / basis_scale
    return [[first * factor, beside * factor], [under * factor, below[1] * factor]]


def emit(values, high, low, to_odd, to_even, to_across, to_sibling):
    for i in range(2):
        to_odd[i], to_even[i] = values[i][0], values[i][1]
        to_across[i], to_sibling[i] = values[0][i], values[1][i]
    for i in range(2):
        for k in range(2):
            high[i, k], low[i, k] = split(values[i][k])


def late_kernel(scale, *refs):
    emit(next_power(scale, *refs[:6], refs[6:8], *refs[8:10]), *refs[10:])


def last_kernel(scale, *refs):
    inputs, refs, outs = refs[:10], refs[10:-4], refs[-4:]
    rows, powers = refs[: SPAN - 1], powers_of(refs[SPAN - 1 :])
    last_high, last_low, keep, send = outs
    values = next_power(scale, *inputs[:6], inputs[6:8], *inputs[8:])
    last = {}
    for i in range(2):
        for k in range(2):
            last[i, k] = split(values[i][k])
            last_high[i, k], last_low[i, k] = last[i, k]
    powers.append([{at: parts[j] for at, parts in last.items()} for j in range(2)])
    pack(inputs[0], [row[...] for row in rows] + [gram_row(powers)], keep, send)


def start_kernel(flags, forcing, *outs):
    field = [[forcing[:, w, s, :] for s in range(2)] for w in range(2)]
    emit(turned(flags[4:5], flags[5:6], field), *outs)


def turned(core, parity, field):
    field = [[select(core, field[1 - i][k], field[i][k]) for k in range(2)] for i in range(2)]
    return [[select(parity, line[1 - k], line[k]) for k in range(2)] for line in field]


PAIR = [shape(2, 2, BLOCK, ROWS, dtype=bf16)] * 2
FACE = shape(2, BLOCK, ROWS)
FIELD = PAIR + [FACE] * 4


def pack(flags, lines, keep, send):
    last = lines[8]
    first_half = jnp.concatenate(
        [last[:, :128], lines[7], jnp.concatenate([lines[6], lines[0]], axis=1)], axis=0
    )
    second_half = jnp.concatenate(
        [
            jnp.concatenate([lines[5], lines[1]], axis=1),
            jnp.concatenate([lines[4], lines[2]], axis=1),
            jnp.concatenate([lines[3], last[:, 128:], jnp.zeros((BLOCK, 48), f32)], axis=1),
        ],
        axis=0,
    )
    core = flags[4:5, :128]
    keep[...] = select(core, second_half, first_half)
    send[...] = select(core, first_half, second_half)


def unpack_gram(first, second):
    lines = [
        first[32:48, 112:],
        second[:16, 96:],
        second[16:32, 80:],
        second[32:48, :64],
        second[16:32, :80],
        second[:16, :96],
        first[32:48, :112],
        first[16:32],
        jnp.concatenate([first[:16], second[32:48, 64:80]], axis=1),
    ]
    lower = jnp.concatenate(
        [
            line
            if line.shape[1] == WIDTH
            else jnp.concatenate([line, jnp.zeros((BLOCK, WIDTH - line.shape[1]), f32)], axis=1)
            for line in lines
        ],
        axis=0,
    )
    row = lax.broadcasted_iota(jnp.int32, (WIDTH, WIDTH), 0) // BLOCK
    column = lax.broadcasted_iota(jnp.int32, (WIDTH, WIDTH), 1) // BLOCK
    return jnp.where(row >= column, lower, lower.T)


def small_solve(gram):
    right = basis_shift * gram[:, :INNER] + basis_scale * gram[:, BLOCK:]
    normal = basis_shift * right[:INNER] + basis_scale * right[BLOCK:]
    target = basis_shift * gram[:INNER, :BLOCK] + basis_scale * gram[BLOCK:, :BLOCK]
    system = jnp.concatenate([normal, target, jnp.zeros((INNER, 48), f32)], axis=1)
    rows = lax.broadcasted_iota(jnp.int32, (INNER, 128), 0)
    group = 8
    for start in range(0, INNER, group):
        columns = [
            jnp.broadcast_to(system[:, start + j : start + j + 1], (INNER, 128))
            for j in range(group)
        ]
        for j in range(group):
            k = start + j
            inverse = 1.0 / columns[j][k : k + 1]
            pivot_row = system[k : k + 1] * inverse
            system = jnp.where(rows == k, pivot_row, system - columns[j] * pivot_row)
            for later in range(j + 1, group):
                scaled = columns[later][k : k + 1] * inverse
                columns[later] = jnp.where(
                    rows == k, scaled, columns[later] - columns[j] * scaled
                )
    coefficients = system[:, INNER:PANEL]
    zero = jnp.zeros((BLOCK, BLOCK), f32)
    update = basis_shift * jnp.concatenate([coefficients, zero], axis=0)
    update = update + basis_scale * jnp.concatenate([zero, coefficients], axis=0)
    return coefficients, update


def add_spread_kernel(own, other, copies):
    copies[...] = jnp.broadcast_to((own[...] + other[...])[None], copies.shape)


def sum_spread_kernel(received, copies):
    copies[...] = jnp.broadcast_to(jnp.sum(received[...], axis=0)[None], copies.shape)


def sum_kernel(received, total):
    total[...] = jnp.sum(received[...], axis=0)


def device_sum(keep, send):
    half = PACKED // 2
    other = lax.ppermute(send, AXES, SIBLING)
    copies = call(add_spread_kernel, "join", shape(16, half, 128), (keep, other), 10**6)
    received = lax.all_to_all(copies, AXES, 0, 0, axis_index_groups=PLANE)
    copies = call(sum_spread_kernel, "resum", shape(8, half, 128), (received,), 10**6)
    received = lax.all_to_all(copies, AXES, 0, 0, axis_index_groups=DEPTH)
    total = call(sum_kernel, "sum", shape(half, 128), (received,), 10**6)
    return total, lax.ppermute(total, AXES, SIBLING)


def dot(left, right, dims=(((1,), (0,)), ((), ()))):
    return lax.dot_general(left, right, dims, precision=highest, preferred_element_type=f32)


def finish_kernel(flags, own, other, *refs):
    powers, (solution_out, residual_out) = powers_of(refs[:-2]), refs[-2:]
    core = flags[4:5, :128]
    own, other = own[...], other[...]
    gram = unpack_gram(select(core, other, own), select(core, own, other))
    coefficients, update = small_solve(gram[:PANEL, :PANEL])
    row = lax.broadcasted_iota(jnp.int32, (BLOCK, PANEL), 0)
    column = lax.broadcasted_iota(jnp.int32, (BLOCK, PANEL), 1)
    identity = jnp.where(row == column, 1.0, 0.0)
    remainder = identity - update.T
    zeros = lambda width: [jnp.zeros((BLOCK, width), f32)] if width else []
    mixing = jnp.concatenate(
        [
            jnp.concatenate(
                zeros(BLOCK * j) + [remainder] + zeros(WIDTH - PANEL - BLOCK * j), axis=1
            )
            for j in range(STEPS + 1)
        ],
        axis=0,
    )
    power = lax.broadcasted_iota(jnp.int32, (PANEL, WIDTH), 1) // BLOCK
    for j in range(STEPS + 1, SPAN):
        mixing = jnp.where(power == j, mixing * GROWTH ** (STEPS - j), mixing)
    second_gram = dot(dot(mixing, gram), mixing, NT)
    second_coefficients, second_update = small_solve(second_gram)
    first_weights = jnp.concatenate([coefficients.T] + zeros(WIDTH - INNER), axis=1)
    second = jnp.concatenate(
        [
            jnp.concatenate([second_coefficients.T] + zeros(BLOCK), axis=1),
            identity - second_update.T,
        ],
        axis=0,
    )
    weights = dot(second, mixing)
    weights = jnp.concatenate([weights[:BLOCK] + first_weights, weights[BLOCK:]], axis=0)
    first, rest = split(weights)
    third = (weights - first.astype(f32) - rest.astype(f32)).astype(bf16)
    parts = jnp.concatenate([first, rest, third], axis=0)
    count = 2 * BLOCK
    plain = (((1,), (0,)), ((), ()))
    mixed = [[None, None], [None, None]]
    for i in range(2):
        for k in range(2):
            highs, lows = stacked(powers, i, k)
            of_high = lax.dot_general(parts, highs, plain, preferred_element_type=f32)
            of_low = lax.dot_general(parts[: 2 * count], lows, plain, preferred_element_type=f32)
            small = of_high[count : 2 * count] + of_low[:count]
            small = small + (of_high[2 * count :] + of_low[count:])
            mixed[i][k] = of_high[:count] + small
    mixed = turned(flags[4:5], flags[5:6], mixed)
    for w in range(2):
        for s in range(2):
            solution_out[:, w, s, :] = mixed[w][s][:BLOCK]
            residual_out[:, w, s, :] = mixed[w][s][BLOCK:]


def on_device(forcing, diag_blocks, coupling):
    wall, stream = lax.axis_index("wall"), lax.axis_index("stream")
    core, parity = wall % 2 > 0, stream % 2 > 0
    across_inside = jnp.where(core, wall < 7, wall > 0)
    odd_inside = jnp.where(parity, stream < 31, stream > 0)
    flags = jnp.stack([across_inside, odd_inside, False, False, core, parity, False, False])
    flags = jnp.broadcast_to(flags.astype(f32)[:, None], (8, ROWS))
    field = call(start_kernel, "start", FIELD, (flags, forcing), 10**6)
    own_parts, corner_parts, even_parts, sibling_parts, late_parts = prepare(diag_blocks, coupling)
    powers, rows = [*field[:2]], []
    for step in range(2 * STEPS):
        to_odd, to_even, to_across, to_sibling = field[2:]
        odd = lax.ppermute(to_odd, AXES, ODD)
        even = lax.ppermute(to_even, AXES, EVEN)
        across = lax.ppermute(to_across, AXES, ACROSS)
        sibling = lax.ppermute(to_sibling, AXES, SIBLING)
        partial, row = call(
            local_kernel,
            "local",
            [shape(2, 2, BLOCK, ROWS), shape(BLOCK, BLOCK * (step + 1))],
            (*own_parts, *powers),
            10**9,
        )
        rows.append(row)
        middle = call(even_kernel, "even", FACE, (partial, even, *even_parts), 10**9)
        operands = (partial, middle, sibling, *sibling_parts)
        below = call(sibling_kernel, "sibling", FACE, operands, 10**9)
        scale = 1.0 if step < STEPS else GROWTH
        operands = (flags, odd, middle, across, below, partial, *corner_parts, *late_parts)
        if step < 2 * STEPS - 1:
            kernel = functools.partial(late_kernel, scale)
            field = call(kernel, "late", FIELD, operands, 10**9)
            powers += field[:2]
    *last, keep, send = call(
        functools.partial(last_kernel, scale),
        "last",
        PAIR + [shape(PACKED // 2, 128)] * 2,
        (*operands, *rows, *powers),
        10**9,
    )
    powers += last
    own, other = device_sum(keep, send)
    return call(
        finish_kernel,
        "finish",
        [jax.ShapeDtypeStruct((BLOCK, 2, 2, ROWS), f32)] * 2,
        (flags, own, other, *powers),
        10**8,
    )


def solution(mesh):
    return jax.shard_map(
        on_device,
        mesh=mesh,
        in_specs=(
            P(None, "wall", "stream", None),
            P("wall", "stream", None, None),
            P(None, "wall", "stream", None, None),
        ),
        out_specs=(P(None, "wall", "stream", None), P(None, "wall", "stream", None)),
        check_vma=False,
    )
```
